512 devices in a mesh: seq: 32 (over z, x), hidden: 16 (over y, core).
Axes of the slice: x: 4, y: 8, z: 8, core: 2. Of those that a mesh axis runs over, the one named last changes fastest.
Arguments:
- tokens: bfloat16 [8192, 8192], P('seq', 'hidden'), may hold values from -6 to 6
- w_first: bfloat16 [64, 128, 128], P('hidden'), may hold values from -0.5 to 0.5
- w_second: bfloat16 [64, 128, 512], P('hidden'), may hold values from -0.5 to 0.5
- w_third: bfloat16 [64, 512, 128], P('hidden'), may hold values from -0.25 to 0.25
- w_fourth: bfloat16 [64, 128, 128], P('hidden'), may hold values from -0.5 to 0.5
- upstream: bfloat16 [8192, 8192], P('seq', 'hidden'), may hold values from -6 to 6
Outputs:
- output: bfloat16 [8192, 8192], P('seq', 'hidden')
- grad_tokens: bfloat16 [8192, 8192], P('seq', 'hidden')
- grad_first: bfloat16 [64, 128, 128], P('hidden')
- grad_second: bfloat16 [64, 128, 512], P('hidden')
- grad_third: bfloat16 [64, 512, 128], P('hidden')
- grad_fourth: bfloat16 [64, 128, 128], P('hidden')
The draws below stay inside these ranges and needn't reach their ends.
All inputs are finite; a program needn't handle non-finite values.
Results may differ from the reference program's by a relative error of at most 0.007.
Values may be sent and summed in bfloat16 or wider, within the bound.
No kernel may reach another device: no remote copies, remote signals or barrier semaphores. Data moves between devices by JAX's collectives and lax.ppermute only.
A program may use at most 64 MiB of HBM per device.

```python
import jax
import jax.numpy as jnp
from jax import lax

NB = 64
BD = 128
BH = 512
D = 8192
PAIR = 2
TOKENS = 8192


def shard_levels(own_key, dims, shards, low, high):
    def one(position, shards_of):
        draws = jax.random.uniform(jax.random.fold_in(jax.random.fold_in(own_key, 6), position), (shards_of,), jnp.float32, low / len(shards), high / len(shards))
        return jnp.repeat(jnp.exp(draws), dims[position] // shards_of).reshape((-1,) + (1,) * (len(dims) - position - 1))

    gain = one(*shards[0])
    for cut in shards[1:]:
        gain = gain * one(*cut)
    return gain


def gaussian(stream_key, shape, width, limit, cuts=(), dtype=jnp.bfloat16):
    array = jax.random.normal(stream_key, shape, jnp.float32) * width
    if len(cuts) > 0:
        array = shard_levels(stream_key, shape, cuts, -0.22, 0.18) * array
    return jnp.clip(array, min=-limit, max=limit).astype(dtype)


def setup_inputs(seed: int = 0) -> dict:
    arg_keys = jax.random.split(jax.random.key(seed), 7)
    tokens = gaussian(arg_keys[0], (TOKENS, D), 1.0, 6.0, ((0, 32), (1, 16)))
    w_first = gaussian(arg_keys[1], (NB, BD, BD), BD ** -0.5, 0.5, ((0, 16),))
    w_second = gaussian(arg_keys[2], (NB, BD, BH), BD ** -0.5, 0.5, ((0, 16),))
    w_third = gaussian(arg_keys[3], (NB, BH, BD), BH ** -0.5, 0.25, ((0, 16),))
    w_fourth = gaussian(arg_keys[4], (NB, BD, BD), BD ** -0.5, 0.5, ((0, 16),))
    upstream = gaussian(arg_keys[5], (TOKENS, D), 1.0, 6.0, ((0, 32), (1, 16)))
    return {"tokens": tokens, "w_first": w_first, "w_second": w_second, "w_third": w_third, "w_fourth": w_fourth, "upstream": upstream}


ROOT = 0.7978845608
CUBIC = 0.044715


def gelu_value(h):
    inner = ROOT * (h + CUBIC * h * h * h)
    return 0.5 * h * (1.0 + jnp.tanh(inner))


def gelu_slope(h):
    slope = jnp.tanh(ROOT * (h + CUBIC * h * h * h))
    return 0.5 * (1.0 + slope) + 0.5 * h * (1.0 - slope * slope) * ROOT * (1.0 + 3.0 * CUBIC * h * h)


def permute(z):
    rows = z.shape[0]
    return z.reshape(rows, NB, NB, PAIR).transpose(0, 2, 1, 3).reshape(rows, NB, BD)


def apply(z, w):
    return jnp.einsum('tbi,bio->tbo', z.astype(jnp.float32), w.astype(jnp.float32))


def apply_t(z, w):
    return jnp.einsum('tbo,bio->tbi', z.astype(jnp.float32), w.astype(jnp.float32))


def outer(left, right):
    return jnp.einsum('tbi,tbo->bio', left.astype(jnp.float32), right.astype(jnp.float32))


def reference(tokens, w_first, w_second, w_third, w_fourth, upstream):
    block = 512 if TOKENS % 512 == 0 else TOKENS
    count = TOKENS // block
    x_all = tokens.reshape(count, block, NB, BD)
    d_all = upstream.reshape(count, block, NB, BD)

    def step(carry, pair_in):
        x, dy = pair_in
        first = apply(x, w_first).astype(jnp.bfloat16)
        mixed = permute(first)
        pre = apply(mixed, w_second)
        act = gelu_value(pre).astype(jnp.bfloat16)
        down = apply(act, w_third).astype(jnp.bfloat16)
        back = permute(down)
        out = apply(back, w_fourth).astype(jnp.bfloat16)
        d_back = apply_t(dy, w_fourth).astype(jnp.bfloat16)
        d_down = permute(d_back)
        d_act = apply_t(d_down, w_third)
        d_pre = (d_act * gelu_slope(pre)).astype(jnp.bfloat16)
        d_mixed = apply_t(d_pre, w_second).astype(jnp.bfloat16)
        d_first = permute(d_mixed)
        dx = apply_t(d_first, w_first).astype(jnp.bfloat16)
        g1, g2, g3, g4 = carry
        g1 = g1 + outer(x, d_first)
        g2 = g2 + outer(mixed, d_pre)
        g3 = g3 + outer(act, d_down)
        g4 = g4 + outer(back, dy)
        return (g1, g2, g3, g4), (out, dx)

    init = (jnp.zeros((NB, BD, BD), jnp.float32), jnp.zeros((NB, BD, BH), jnp.float32),
            jnp.zeros((NB, BH, BD), jnp.float32), jnp.zeros((NB, BD, BD), jnp.float32))
    grads, outs = lax.scan(step, init, (x_all, d_all))
    scale = jnp.float32(TOKENS) ** -0.5
    output = outs[0].reshape(TOKENS, D)
    grad_tokens = outs[1].reshape(TOKENS, D)
    return (output, grad_tokens, (grads[0] * scale).astype(jnp.bfloat16), (grads[1] * scale).astype(jnp.bfloat16),
            (grads[2] * scale).astype(jnp.bfloat16), (grads[3] * scale).astype(jnp.bfloat16))
```

```python
import functools

import jax
import jax.numpy as jnp
from jax import lax
from jax.experimental import pallas as pl
from jax.experimental.pallas import tpu as pltpu
from jax.sharding import Mesh, PartitionSpec as P

ROOT = 0.7978845608
CUBIC = 0.044715
BF = jnp.bfloat16
F32 = jnp.float32
PAIR = 2
NN = (((1,), (0,)), ((), ()))
NT = (((1,), (1,)), ((), ()))
TN = (((0,), (0,)), ((), ()))
TT = (((0,), (1,)), ((), ()))


def dot(a, b, dims):
    return lax.dot_general(a, b, dims, preferred_element_type=F32)


def call(kernel, outs, *args, flops=0, transcendentals=0):
    moved = sum(a.size * a.dtype.itemsize for a in (*args, *outs))
    return pl.pallas_call(
        kernel,
        out_shape=outs,
        compiler_params=pltpu.CompilerParams(vmem_limit_bytes=24 * 1024 * 1024),
        cost_estimate=pl.CostEstimate(
            flops=int(flops), bytes_accessed=int(moved), transcendentals=int(transcendentals)
        ),
    )(*args)


def shape(*dims, dtype=BF):
    return jax.ShapeDtypeStruct(dims, dtype)


def place(send, slot, low, high, groups):
    width, tokens = low.shape
    per = width // groups
    both = jnp.concatenate(
        [low.reshape(groups, per, tokens), high.reshape(groups, per, tokens)], axis=1
    )
    send[:, slot * 2 * per : (slot + 1) * 2 * per, :] = both.astype(BF)


def enter_kernel(groups, x, dy, w1, w4, send):
    local, width, _ = w1.shape
    half = local // 2
    for k in range(half):
        pair = []
        for b in (2 * k, 2 * k + 1):
            cols = pl.ds(b * width, width)
            pair.append(dot(w1[b], x[:, cols], TT))
        place(send, k, *pair, groups)
    for k in range(half):
        pair = []
        for b in (2 * k, 2 * k + 1):
            cols = pl.ds(b * width, width)
            pair.append(dot(w4[b], dy[:, cols], NT))
        place(send, half + k, *pair, groups)


def source_row(r, local, groups):
    per = local * PAIR
    own, rest = r // (groups * per), r % (groups * per)
    group, rest = rest // per, rest % per
    theirs, one = rest // PAIR, rest % PAIR
    return group * (local * per) + theirs * per + own * PAIR + one


def ready_kernel(groups, w2, w3, order, order_t, w2t, w3t):
    local = w2.shape[0]
    n = order.shape[0]
    source = source_row(lax.broadcasted_iota(jnp.int32, (n, 1), 0), local, groups)
    order[...] = (lax.broadcasted_iota(jnp.int32, (n, n), 1) == source).astype(F32).astype(BF)
    source = source_row(lax.broadcasted_iota(jnp.int32, (1, n), 1), local, groups)
    order_t[...] = (lax.broadcasted_iota(jnp.int32, (n, n), 0) == source).astype(F32).astype(BF)
    for b in range(local):
        w2t[b] = w2[b].T
        w3t[b] = w3[b].T


def middle_kernel(groups, got, order, w2, w3, w2t, w3t, send, mixed, d_down, act, d_pre):
    local, width, _ = w2.shape
    rows = got.shape[1] // 2
    n, tokens = order.shape[0], got.shape[2]
    mixed[...] = dot(order[...], got[:, :rows, :].reshape(n, tokens), NN).astype(BF)
    d_down[...] = dot(order[...], got[:, rows:, :].reshape(n, tokens), NN).astype(BF)
    downs, d_mixeds = [], []
    for b in range(local):
        part = pl.ds(b * width, width)
        h = dot(w2t[b], mixed[part, :], NN)
        squared = h * h
        slope = jnp.tanh(ROOT * (h + CUBIC * (squared * h)))
        act[b] = (0.5 * h * (1.0 + slope)).astype(BF)
        downs.append(dot(w3t[b], act[b], NN))
        d_act = dot(w3[b], d_down[part, :], NN)
        gain = 0.5 * (1.0 + slope) + 0.5 * h * (1.0 - slope * slope) * ROOT * (
            1.0 + 3.0 * CUBIC * squared
        )
        d_pre[b] = (d_act * gain).astype(BF)
        d_mixeds.append(dot(w2[b], d_pre[b], NN))
        if b % 2 == 1:
            place(send, b // 2, *downs, groups)
            place(send, (local + b) // 2, *d_mixeds, groups)
            downs, d_mixeds = [], []


def wide_grads_kernel(mixed, d_down, act, d_pre, grads):
    local, hidden, _ = act.shape
    width = mixed.shape[0] // local
    parts = hidden // width
    for b in range(local):
        rows = pl.ds(b * width, width)
        second = dot(mixed[rows, :], d_pre[b], NT).astype(BF)
        third = dot(act[b], d_down[rows, :], NT).astype(BF)
        for j in range(parts):
            part = slice(j * width, (j + 1) * width)
            grads[j, b * width : (b + 1) * width, :] = second[:, part]
            grads[parts + j, b * width : (b + 1) * width, :] = third[part, :]


def leave_kernel(got, order_t, x, dy, wide, back, d_first, grads):
    rows = got.shape[1] // 2
    n, tokens = order_t.shape[0], got.shape[2]
    parts, high, width = wide.shape
    grads[:, :high, :] = wide[...]
    local = n // width
    back[...] = dot(got[:, :rows, :].reshape(n, tokens), order_t[...], TN).astype(BF)
    d_first[...] = dot(got[:, rows:, :].reshape(n, tokens), order_t[...], TN).astype(BF)
    for b in range(local):
        cols = pl.ds(b * width, width)
        grads[b, high:, :] = dot(x[:, cols], d_first[:, cols], TN).astype(BF)
        grads[local + b, high:, :] = dot(back[:, cols], dy[:, cols], TN).astype(BF)


def outputs_kernel(back, d_first, w1, w4, output, grad_tokens):
    local, width, _ = w1.shape
    for b in range(local):
        cols = pl.ds(b * width, width)
        output[:, cols] = dot(back[:, cols], w4[b], NN).astype(BF)
        grad_tokens[:, cols] = dot(d_first[:, cols], w1[b], NT).astype(BF)


def add_kernel(got, total):
    acc = got[0].astype(F32)
    for k in range(1, got.shape[0]):
        acc = acc + got[k].astype(F32)
    total[...] = acc.astype(BF)


def add_copy_kernel(scale, got, copies):
    acc = got[0].astype(F32)
    for k in range(1, got.shape[0]):
        acc = acc + got[k].astype(F32)
    total = (acc * scale).astype(BF)
    for k in range(copies.shape[0]):
        copies[k] = total


def unpack_kernel(got, first, second, third, fourth):
    local, width, hidden = second.shape
    parts = hidden // width
    for b in range(local):
        rows = slice(b * width, (b + 1) * width)
        for j in range(parts):
            part = slice(j * width, (j + 1) * width)
            second[b, :, part] = got[j, rows, :]
            third[b, part, :] = got[parts + j, rows, :]
        first[b] = got[b, local * width :, :]
        fourth[b] = got[local + b, local * width :, :]


def exchange(value, axes):
    return lax.all_to_all(value, axes, split_axis=0, concat_axis=0, tiled=True)


def body(near, far, all_tokens, tokens, w_first, w_second, w_third, w_fourth, upstream):
    count, wide = tokens.shape
    local, width, hidden = w_second.shape
    groups = lax.axis_size("hidden")
    parts = 2 * hidden // width
    scale = float(all_tokens) ** -0.5
    rows = 2 * local * local * PAIR
    send = call(
        functools.partial(enter_kernel, groups),
        [shape(groups, rows, count)],
        tokens, upstream, w_first, w_fourth,
        flops=4 * count * wide * width,
    )[0]
    got = exchange(send, "hidden")
    order, order_t, w2t, w3t = call(
        functools.partial(ready_kernel, groups),
        [shape(wide, wide), shape(wide, wide), shape(local, hidden, width), shape(local, width, hidden)],
        w_second, w_third,
        flops=2e8,
    )
    send, mixed, d_down, act, d_pre = call(
        functools.partial(middle_kernel, groups),
        [
            shape(groups, rows, count), shape(wide, count), shape(wide, count),
            shape(local, hidden, count), shape(local, hidden, count),
        ],
        got, order, w_second, w_third, w2t, w3t,
        flops=8 * count * wide * hidden, transcendentals=count * local * hidden,
    )
    got = exchange(send, "hidden")
    (grads,) = call(
        wide_grads_kernel, [shape(parts, local * width, width)],
        mixed, d_down, act, d_pre,
        flops=4 * count * wide * hidden,
    )
    back, d_first, grads = call(
        leave_kernel,
        [shape(count, wide), shape(count, wide), shape(parts, (local + 1) * width, width)],
        got, order_t, tokens, upstream, grads,
        flops=4 * count * wide * (wide + width),
    )
    got = exchange(grads, near)
    output, grad_tokens = call(
        outputs_kernel, [shape(count, wide), shape(count, wide)],
        back, d_first, w_first, w_fourth,
        flops=4 * count * wide * width,
    )
    (total,) = call(add_kernel, [shape((local + 1) * width, width)], got, flops=got.size)
    got = lax.all_gather(total, far, axis=0, tiled=False)
    (copies,) = call(
        functools.partial(add_copy_kernel, scale),
        [shape(parts, (local + 1) * width, width)], got, flops=got.size,
    )
    got = exchange(copies, near)
    first, second, third, fourth = call(
        unpack_kernel,
        [shape(*w.shape) for w in (w_first, w_second, w_third, w_fourth)],
        got,
    )
    return output, grad_tokens, first, second, third, fourth


def solution(mesh):
    seq, groups = mesh.shape["seq"], mesh.shape["hidden"]
    near_size = 8
    fine = Mesh(
        mesh.devices.reshape(seq // near_size, near_size, groups), ("far", "near", "hidden")
    )
    rows = P(("far", "near"), "hidden")
    weight = P("hidden", None, None)

    def run(tokens, w_first, w_second, w_third, w_fourth, upstream):
        return jax.shard_map(
            functools.partial(body, "near", "far", tokens.shape[0]),
            mesh=fine,
            in_specs=(rows, weight, weight, weight, weight, rows),
            out_specs=(rows, rows, weight, weight, weight, weight),
            check_vma=False,
        )(tokens, w_first, w_second, w_third, w_fourth, upstream)

    return run
```

```python
import functools

import jax
import jax.numpy as jnp
from jax import lax
from jax.experimental import pallas as pl
from jax.experimental.pallas import tpu as pltpu
from jax.sharding import Mesh, PartitionSpec as P

ROOT = 0.7978845608
CUBIC = 0.044715
BF = jnp.bfloat16
F32 = jnp.float32
PAIR = 2
NN = (((1,), (0,)), ((), ()))
NT = (((1,), (1,)), ((), ()))
TN = (((0,), (0,)), ((), ()))
TT = (((0,), (1,)), ((), ()))


def dot(a, b, dims):
    return lax.dot_general(a, b, dims, preferred_element_type=F32)


def call(kernel, outs, *args, flops=0, transcendentals=0, vmem=24 << 20, **more):
    moved = sum(a.size * a.dtype.itemsize for a in (*args, *outs))
    return pl.pallas_call(
        kernel,
        out_shape=outs,
        compiler_params=pltpu.CompilerParams(vmem_limit_bytes=vmem),
        cost_estimate=pl.CostEstimate(
            flops=int(flops), bytes_accessed=int(moved), transcendentals=int(transcendentals)
        ),
        **more,
    )(*args)


def shape(*dims, dtype=BF):
    return jax.ShapeDtypeStruct(dims, dtype)


def place(send, slot, low, high, groups):
    width, tokens = low.shape
    per = width // groups
    both = jnp.concatenate(
        [low.reshape(groups, per, tokens), high.reshape(groups, per, tokens)], axis=1
    )
    send[:, slot * 2 * per : (slot + 1) * 2 * per, :] = both.astype(BF)


def enter_kernel(groups, x_in, w1_in, dy_in, w4_in, send, x, w1, dy, w4, arrived):
    copies = [
        pltpu.make_async_copy(source, target, arrived.at[k])
        for k, (source, target) in enumerate(((x_in, x), (w1_in, w1), (dy_in, dy), (w4_in, w4)))
    ]
    for copy in copies:
        copy.start()
    local, width, _ = w1.shape
    half = local // 2
    copies[0].wait()
    copies[1].wait()
    for k in range(half):
        pair = []
        for b in (2 * k, 2 * k + 1):
            cols = pl.ds(b * width, width)
            pair.append(dot(w1[b], x[:, cols], TT))
        place(send, k, *pair, groups)
    copies[2].wait()
    copies[3].wait()
    for k in range(half):
        pair = []
        for b in (2 * k, 2 * k + 1):
            cols = pl.ds(b * width, width)
            pair.append(dot(w4[b], dy[:, cols], NT))
        place(send, half + k, *pair, groups)


def gather_blocks(got, low, local, out):
    groups, _, tokens = got.shape
    per = local * PAIR
    held = local * per
    n = out.shape[0] // local
    some = n // held
    r = lax.broadcasted_iota(jnp.int32, (n, 1), 0)
    own, group = r // (some * per), (r // per) % some
    theirs, one = (r // PAIR) % local, r % PAIR
    source = group * held + theirs * per + own * PAIR + one
    order = (lax.broadcasted_iota(jnp.int32, (n, n), 1) == source).astype(F32).astype(BF)
    for k in range(groups // some):
        rows = got[k * some : (k + 1) * some, low : low + held, :].reshape(n, tokens)
        moved = dot(order, rows, NN).astype(BF)
        for b in range(local):
            at = b * n + k * some * per
            out[at : at + some * per, :] = moved[b * some * per : (b + 1) * some * per, :]


def middle_kernel(groups, got, w2, w3, send, grads, mixed, d_down):
    local, width, hidden = w2.shape
    parts = hidden // width
    gather_blocks(got, 0, local, mixed)
    gather_blocks(got, got.shape[1] // 2, local, d_down)
    downs, d_mixeds = [], []
    for b in range(local):
        rows = pl.ds(b * width, width)
        h = dot(w2[b], mixed[rows, :], TN)
        squared = h * h
        half = 0.5 + 0.5 * jnp.tanh(h * (ROOT + (ROOT * CUBIC) * squared))
        act = (h * half).astype(BF)
        gain = half + h * (half - half * half) * (2.0 * ROOT + (6.0 * ROOT * CUBIC) * squared)
        d_act = dot(w3[b], d_down[rows, :], NN)
        d_pre = (d_act * gain).astype(BF)
        downs.append(dot(w3[b], act, TN))
        d_mixeds.append(dot(w2[b], d_pre, NN))
        if b % 2 == 1:
            place(send, b // 2, *downs, groups)
            place(send, (local + b) // 2, *d_mixeds, groups)
            downs, d_mixeds = [], []
        second = dot(mixed[rows, :], d_pre, NT).astype(BF)
        third = dot(act, d_down[rows, :], NT).astype(BF)
        for j in range(parts):
            part = slice(j * width, (j + 1) * width)
            grads[j, b * width : (b + 1) * width, :] = second[:, part]
            grads[parts + j, b * width : (b + 1) * width, :] = third[part, :]


def leave_kernel(got, x, dy, wide, back, d_first, grads):
    parts, high, width = wide.shape
    local = high // width
    grads[:, :high, :] = wide[...]
    gather_blocks(got, 0, local, back)
    gather_blocks(got, got.shape[1] // 2, local, d_first)
    for b in range(local):
        rows = pl.ds(b * width, width)
        grads[b, high:, :] = dot(x[:, rows], d_first[rows, :], TT).astype(BF)
        grads[local + b, high:, :] = dot(back[rows, :], dy[:, rows], NN).astype(BF)


def outputs_kernel(back, d_first, w1, w4, output, grad_tokens):
    local, width, _ = w1.shape
    for b in range(local):
        cols = pl.ds(b * width, width)
        output[:, cols] = dot(back[cols, :], w4[b], TN).astype(BF)
        grad_tokens[:, cols] = dot(d_first[cols, :], w1[b], TT).astype(BF)


def add_kernel(got, total):
    acc = got[0].astype(F32)
    for k in range(1, got.shape[0]):
        acc = acc + got[k].astype(F32)
    total[...] = acc.astype(BF)


def add_copy_kernel(scale, got, copies):
    acc = got[0].astype(F32)
    for k in range(1, got.shape[0]):
        acc = acc + got[k].astype(F32)
    total = (acc * scale).astype(BF)
    for k in range(copies.shape[0]):
        copies[k] = total


def unpack_kernel(got, first, second, third, fourth):
    local, width, hidden = second.shape
    parts = hidden // width
    for b in range(local):
        rows = slice(b * width, (b + 1) * width)
        for j in range(parts):
            part = slice(j * width, (j + 1) * width)
            second[b, :, part] = got[j, rows, :]
            third[b, part, :] = got[parts + j, rows, :]
        first[b] = got[b, local * width :, :]
        fourth[b] = got[local + b, local * width :, :]


def exchange(value, axes):
    return lax.all_to_all(value, axes, split_axis=0, concat_axis=0, tiled=True)


def body(near, far, all_tokens, tokens, w_first, w_second, w_third, w_fourth, upstream):
    count, wide = tokens.shape
    local, width, hidden = w_second.shape
    groups = lax.axis_size("hidden")
    parts = 2 * hidden // width
    scale = float(all_tokens) ** -0.5
    rows = 2 * local * local * PAIR
    entering = (tokens, w_first, upstream, w_fourth)
    (send,) = call(
        functools.partial(enter_kernel, groups),
        [shape(groups, rows, count)],
        *entering,
        flops=4 * count * wide * width, vmem=60 << 20,
        in_specs=[pl.BlockSpec(memory_space=pltpu.HBM)] * 4,
        scratch_shapes=[pltpu.VMEM(a.shape, BF) for a in entering]
        + [pltpu.SemaphoreType.DMA((4,))],
    )
    got = exchange(send, "hidden")
    send, grads = call(
        functools.partial(middle_kernel, groups),
        [shape(groups, rows, count), shape(parts, local * width, width)],
        got, w_second, w_third,
        flops=12 * count * wide * hidden, transcendentals=count * local * hidden,
        scratch_shapes=[pltpu.VMEM((wide, count), BF)] * 2,
    )
    got = exchange(send, "hidden")
    back, d_first, grads = call(
        leave_kernel,
        [shape(wide, count), shape(wide, count), shape(parts, (local + 1) * width, width)],
        got, tokens, upstream, grads,
        flops=8 * count * wide * width,
    )
    got = exchange(grads, near)
    output, grad_tokens = call(
        outputs_kernel, [shape(count, wide), shape(count, wide)],
        back, d_first, w_first, w_fourth,
        flops=4 * count * wide * width,
    )
    (total,) = call(add_kernel, [shape((local + 1) * width, width)], got, flops=got.size)
    got = lax.all_gather(total, far, axis=0, tiled=False)
    (copies,) = call(
        functools.partial(add_copy_kernel, scale),
        [shape(parts, (local + 1) * width, width)], got, flops=got.size,
    )
    got = exchange(copies, near)
    first, second, third, fourth = call(
        unpack_kernel,
        [shape(*w.shape) for w in (w_first, w_second, w_third, w_fourth)],
        got,
    )
    return output, grad_tokens, first, second, third, fourth


def solution(mesh):
    seq, groups = mesh.shape["seq"], mesh.shape["hidden"]
    near_size = 8
    fine = Mesh(
        mesh.devices.reshape(seq // near_size, near_size, groups), ("far", "near", "hidden")
    )
    rows = P(("far", "near"), "hidden")
    weight = P("hidden", None, None)

    def run(tokens, w_first, w_second, w_third, w_fourth, upstream):
        return jax.shard_map(
            functools.partial(body, "near", "far", tokens.shape[0]),
            mesh=fine,
            in_specs=(rows, weight, weight, weight, weight, rows),
            out_specs=(rows, rows, weight, weight, weight, weight),
            check_vma=False,
        )(tokens, w_first, w_second, w_third, w_fourth, upstream)

    return run
```

```python
import functools

import jax
import jax.numpy as jnp
from jax import lax
from jax.experimental import pallas as pl
from jax.experimental.pallas import tpu as pltpu
from jax.sharding import Mesh, PartitionSpec as P

ROOT = 0.7978845608
CUBIC = 0.044715
BF = jnp.bfloat16
F32 = jnp.float32
PAIR = 2
NN = (((1,), (0,)), ((), ()))
NT = (((1,), (1,)), ((), ()))
TN = (((0,), (0,)), ((), ()))
TT = (((0,), (1,)), ((), ()))


def dot(a, b, dims):
    return lax.dot_general(a, b, dims, preferred_element_type=F32)


def call(kernel, outs, *args, flops=0, transcendentals=0, vmem=24 << 20, **more):
    moved = sum(a.size * a.dtype.itemsize for a in (*args, *outs))
    return pl.pallas_call(
        kernel,
        out_shape=outs,
        compiler_params=pltpu.CompilerParams(vmem_limit_bytes=vmem),
        cost_estimate=pl.CostEstimate(
            flops=int(flops), bytes_accessed=int(moved), transcendentals=int(transcendentals)
        ),
        **more,
    )(*args)


def shape(*dims, dtype=BF):
    return jax.ShapeDtypeStruct(dims, dtype)


def place(send, slot, low, high, groups):
    width, tokens = low.shape
    per = width // groups
    both = jnp.concatenate(
        [low.reshape(groups, per, tokens), high.reshape(groups, per, tokens)], axis=1
    )
    send[:, slot * 2 * per : (slot + 1) * 2 * per, :] = both.astype(BF)


def enter_kernel(groups, x_in, w1_in, dy_in, w4_in, out, x, w1, dy, w4, send, arrived, left):
    copies = [
        pltpu.make_async_copy(source, target, arrived.at[k])
        for k, (source, target) in enumerate(((x_in, x), (w1_in, w1), (dy_in, dy), (w4_in, w4)))
    ]
    for copy in copies:
        copy.start()
    local, width, _ = w1.shape
    slots = local // 2
    per = send.shape[1] // (2 * slots)
    leaving = []
    for k in range(2 * slots):
        if k % slots == 0:
            copies[k // slots * 2].wait()
            copies[k // slots * 2 + 1].wait()
        pair = []
        for b in (2 * (k % slots), 2 * (k % slots) + 1):
            cols = pl.ds(b * width, width)
            if k < slots:
                pair.append(dot(w1[b], x[:, cols], TT))
            else:
                pair.append(dot(w4[b], dy[:, cols], NT))
        place(send, k, *pair, groups)
        rows = pl.ds(k * per, per)
        copy = pltpu.make_async_copy(send.at[:, rows, :], out.at[:, rows, :], left.at[k])
        copy.start()
        leaving.append(copy)
    for copy in leaving:
        copy.wait()


def gather_blocks(got, low, local, out):
    groups, _, tokens = got.shape
    per = local * PAIR
    held = local * per
    n = out.shape[0] // local
    some = n // held
    r = lax.broadcasted_iota(jnp.int32, (n, 1), 0)
    own, group = r // (some * per), (r // per) % some
    theirs, one = (r // PAIR) % local, r % PAIR
    source = group * held + theirs * per + own * PAIR + one
    order = (lax.broadcasted_iota(jnp.int32, (n, n), 1) == source).astype(F32).astype(BF)
    for k in range(groups // some):
        rows = got[k * some : (k + 1) * some, low : low + held, :].reshape(n, tokens)
        moved = dot(order, rows, NN).astype(BF)
        for b in range(local):
            at = b * n + k * some * per
            out[at : at + some * per, :] = moved[b * some * per : (b + 1) * some * per, :]


def middle_kernel(groups, got, w2, w3, send, grads, mixed, d_down):
    local, width, hidden = w2.shape
    parts = hidden // width
    gather_blocks(got, 0, local, mixed)
    gather_blocks(got, got.shape[1] // 2, local, d_down)
    downs, d_mixeds = [], []
    for b in range(local):
        rows = pl.ds(b * width, width)
        h = dot(w2[b], mixed[rows, :], TN)
        squared = h * h
        half = 0.5 + 0.5 * jnp.tanh(h * (ROOT + (ROOT * CUBIC) * squared))
        act = (h * half).astype(BF)
        gain = half + h * (half - half * half) * (2.0 * ROOT + (6.0 * ROOT * CUBIC) * squared)
        d_act = dot(w3[b], d_down[rows, :], NN)
        d_pre = (d_act * gain).astype(BF)
        downs.append(dot(w3[b], act, TN))
        d_mixeds.append(dot(w2[b], d_pre, NN))
        if b % 2 == 1:
            place(send, b // 2, *downs, groups)
            place(send, (local + b) // 2, *d_mixeds, groups)
            downs, d_mixeds = [], []
        second = dot(mixed[rows, :], d_pre, NT).astype(BF)
        third = dot(act, d_down[rows, :], NT).astype(BF)
        for j in range(parts):
            part = slice(j * width, (j + 1) * width)
            grads[j, b * width : (b + 1) * width, :] = second[:, part]
            grads[parts + j, b * width : (b + 1) * width, :] = third[part, :]


def leave_kernel(got, x, dy, wide, back, d_first, grads):
    parts, high, width = wide.shape
    local = high // width
    grads[:, :high, :] = wide[...]
    gather_blocks(got, 0, local, back)
    gather_blocks(got, got.shape[1] // 2, local, d_first)
    for b in range(local):
        rows = pl.ds(b * width, width)
        grads[b, high:, :] = dot(x[:, rows], d_first[rows, :], TT).astype(BF)
        grads[local + b, high:, :] = dot(back[rows, :], dy[:, rows], NN).astype(BF)


def outputs_kernel(back, d_first, w1, w4, output, grad_tokens):
    local, width, _ = w1.shape
    for b in range(local):
        cols = pl.ds(b * width, width)
        output[:, cols] = dot(back[cols, :], w4[b], TN).astype(BF)
        grad_tokens[:, cols] = dot(d_first[cols, :], w1[b], TT).astype(BF)


def add_kernel(got, total):
    acc = got[0].astype(F32)
    for k in range(1, got.shape[0]):
        acc = acc + got[k].astype(F32)
    total[...] = acc.astype(BF)


def add_copy_kernel(scale, got, copies, total, left):
    acc = got[0].astype(F32)
    for k in range(1, got.shape[0]):
        acc = acc + got[k].astype(F32)
    total[...] = (acc * scale).astype(BF)
    leaving = [
        pltpu.make_async_copy(total, copies.at[k], left.at[k]) for k in range(copies.shape[0])
    ]
    for copy in leaving:
        copy.start()
    for copy in leaving:
        copy.wait()


def unpack_kernel(got, first, second, third, fourth, done):
    local, width, hidden = second.shape
    parts = hidden // width
    pairs = []
    for j in range(parts):
        part = pl.ds(j * width, width)
        pairs.append((got.at[j, :local], second.at[:, :, part]))
        pairs.append((got.at[parts + j, :local], third.at[:, part, :]))
    pairs.append((got.at[:local, local], first))
    pairs.append((got.at[local:, local], fourth))
    copies = [
        pltpu.make_async_copy(source, target, done.at[k])
        for k, (source, target) in enumerate(pairs)
    ]
    for copy in copies:
        copy.start()
    for copy in copies:
        copy.wait()


def exchange(value, axes):
    return lax.all_to_all(value, axes, split_axis=0, concat_axis=0, tiled=True)


def body(near, far, all_tokens, tokens, w_first, w_second, w_third, w_fourth, upstream):
    count, wide = tokens.shape
    local, width, hidden = w_second.shape
    groups = lax.axis_size("hidden")
    parts = 2 * hidden // width
    scale = float(all_tokens) ** -0.5
    rows = 2 * local * local * PAIR
    entering = (tokens, w_first, upstream, w_fourth)
    (send,) = call(
        functools.partial(enter_kernel, groups),
        [shape(groups, rows, count)],
        *entering,
        flops=4 * count * wide * width, vmem=60 << 20,
        in_specs=[pl.BlockSpec(memory_space=pl.ANY)] * 4,
        out_specs=[pl.BlockSpec(memory_space=pl.ANY)],
        scratch_shapes=[pltpu.VMEM(a.shape, BF) for a in entering]
        + [pltpu.VMEM((groups, rows, count), BF)]
        + [pltpu.SemaphoreType.DMA((4,)), pltpu.SemaphoreType.DMA((local,))],
    )
    got = exchange(send, "hidden")
    send, grads = call(
        functools.partial(middle_kernel, groups),
        [shape(groups, rows, count), shape(parts, local * width, width)],
        got, w_second, w_third,
        flops=12 * count * wide * hidden, transcendentals=count * local * hidden,
        scratch_shapes=[pltpu.VMEM((wide, count), BF)] * 2,
    )
    got = exchange(send, "hidden")
    back, d_first, grads = call(
        leave_kernel,
        [shape(wide, count), shape(wide, count), shape(parts, (local + 1) * width, width)],
        got, tokens, upstream, grads,
        flops=8 * count * wide * width,
    )
    got = exchange(grads, near)
    output, grad_tokens = call(
        outputs_kernel, [shape(count, wide), shape(count, wide)],
        back, d_first, w_first, w_fourth,
        flops=4 * count * wide * width,
    )
    (total,) = call(add_kernel, [shape((local + 1) * width, width)], got, flops=got.size)
    got = lax.all_gather(total, far, axis=0, tiled=False)
    (copies,) = call(
        functools.partial(add_copy_kernel, scale),
        [shape(parts, (local + 1) * width, width)],
        got,
        flops=got.size,
        out_specs=[pl.BlockSpec(memory_space=pl.ANY)],
        scratch_shapes=[
            pltpu.VMEM(((local + 1) * width, width), BF), pltpu.SemaphoreType.DMA((parts,)),
        ],
    )
    got = exchange(copies, near).reshape(parts, local + 1, width, width)
    first, second, third, fourth = call(
        unpack_kernel,
        [shape(*w.shape) for w in (w_first, w_second, w_third, w_fourth)],
        got,
        in_specs=[pl.BlockSpec(memory_space=pl.ANY)],
        out_specs=[pl.BlockSpec(memory_space=pl.ANY)] * 4,
        scratch_shapes=[pltpu.SemaphoreType.DMA((parts + 2,))],
    )
    return output, grad_tokens, first, second, third, fourth


def solution(mesh):
    seq, groups = mesh.shape["seq"], mesh.shape["hidden"]
    near_size = 8
    fine = Mesh(
        mesh.devices.reshape(seq // near_size, near_size, groups), ("far", "near", "hidden")
    )
    rows = P(("far", "near"), "hidden")
    weight = P("hidden", None, None)

    def run(tokens, w_first, w_second, w_third, w_fourth, upstream):
        return jax.shard_map(
            functools.partial(body, "near", "far", tokens.shape[0]),
            mesh=fine,
            in_specs=(rows, weight, weight, weight, weight, rows),
            out_specs=(rows, rows, weight, weight, weight, weight),
            check_vma=False,
        )(tokens, w_first, w_second, w_third, w_fourth, upstream)

    return run
```

```python
import functools

import jax
import jax.numpy as jnp
from jax import lax
from jax.experimental import pallas as pl
from jax.experimental.pallas import tpu as pltpu
from jax.sharding import Mesh, PartitionSpec as P

ROOT = 0.7978845608
CUBIC = 0.044715
BF = jnp.bfloat16
F32 = jnp.float32
PAIR = 2
Z_LOW = 2
X_SIZE = 4
NN = (((1,), (0,)), ((), ()))
NT = (((1,), (1,)), ((), ()))
TN = (((0,), (0,)), ((), ()))
TT = (((0,), (1,)), ((), ()))


def dot(a, b, dims):
    return lax.dot_general(a, b, dims, preferred_element_type=F32)


def call(kernel, outs, *args, flops=0, transcendentals=0, vmem=24 << 20, **more):
    moved = sum(a.size * a.dtype.itemsize for a in (*args, *outs))
    return pl.pallas_call(
        kernel,
        out_shape=outs,
        compiler_params=pltpu.CompilerParams(vmem_limit_bytes=vmem),
        cost_estimate=pl.CostEstimate(
            flops=int(flops), bytes_accessed=int(moved), transcendentals=int(transcendentals)
        ),
        **more,
    )(*args)


def shape(*dims, dtype=BF):
    return jax.ShapeDtypeStruct(dims, dtype)


def stack(low, high):
    width, tokens = low.shape
    per = 2 * PAIR * Z_LOW
    split = (width // per, per, tokens)
    return jnp.concatenate([low.reshape(split), high.reshape(split)], axis=1)


def enter_kernel(groups, x_in, w1_in, dy_in, w4_in, send, x, w1, dy, w4, arrived):
    copies = [
        pltpu.make_async_copy(source, target, arrived.at[k])
        for k, (source, target) in enumerate(((x_in, x), (w1_in, w1), (dy_in, dy), (w4_in, w4)))
    ]
    for copy in copies:
        copy.start()
    local, width, _ = w1.shape
    tokens = x.shape[0]
    per = width // groups
    rows = local * per // Z_LOW
    first_half = lax.broadcasted_iota(jnp.int32, (groups, per, tokens), 1) < per // 2
    for k in range(2):
        copies[2 * k].wait()
        copies[2 * k + 1].wait()
        to_zl = [[], []]
        for pair in range(local // 2):
            both = []
            for b in (2 * pair, 2 * pair + 1):
                cols = pl.ds(b * width, width)
                if k == 0:
                    z = dot(w1[b], x[:, cols], TT)
                else:
                    z = dot(w4[b], dy[:, cols], NT)
                both.append(z.reshape(groups, per, tokens))
            low, high = both
            to_zl[0].append(jnp.where(first_half, low, pltpu.roll(high, per // 2, 1)))
            to_zl[1].append(jnp.where(first_half, pltpu.roll(low, per // 2, 1), high))
        for zl in range(Z_LOW):
            filled = jnp.concatenate(to_zl[zl], axis=1).astype(BF)
            send[zl * groups : (zl + 1) * groups, k * rows : (k + 1) * rows, :] = filled


def one_hot(source):
    n = source.shape[0]
    return (lax.broadcasted_iota(jnp.int32, (n, n), 1) == source).astype(F32).astype(BF)


def collect(got, k, theirs, out):
    count, rows, tokens = got.shape
    groups, held = count // Z_LOW, rows // 2
    mine = held // (theirs * PAIR)
    n = out.shape[0] // mine
    some = n // held
    per = theirs * PAIR
    r = lax.broadcasted_iota(jnp.int32, (n, 1), 0)
    own, group = r // (some * per), (r // per) % some
    their, one = (r // PAIR) % theirs, r % PAIR
    order = one_hot(group * held + their * (mine * PAIR) + own * PAIR + one)
    for zl in range(Z_LOW):
        for g in range(groups // some):
            at = zl * groups + g * some
            taken = got[at : at + some, k * held : (k + 1) * held, :].reshape(n, tokens)
            moved = dot(order, taken, NN).astype(BF)
            for b in range(mine):
                to = b * n + g * some * per
                out[to : to + some * per, zl * tokens : (zl + 1) * tokens] = moved[
                    b * some * per : (b + 1) * some * per, :
                ]


def collect_back(got, k, local, out):
    count, rows, tokens = got.shape
    groups, held = count // Z_LOW, rows // 2
    theirs = held // (local * PAIR)
    n = out.shape[0] // local
    some = n // (Z_LOW * held)
    per = Z_LOW * theirs * PAIR
    r = lax.broadcasted_iota(jnp.int32, (n, 1), 0)
    own, group = r // (some * per), (r // per) % some
    zl, their, one = (r // (theirs * PAIR)) % Z_LOW, (r // PAIR) % theirs, r % PAIR
    order = one_hot((zl * some + group) * held + their * (local * PAIR) + own * PAIR + one)
    for g in range(groups // some):
        taken = jnp.concatenate(
            [
                got[z * groups + g * some : z * groups + (g + 1) * some, k * held : (k + 1) * held, :]
                .reshape(some * held, tokens)
                for z in range(Z_LOW)
            ],
            axis=0,
        )
        moved = dot(order, taken, NN).astype(BF)
        for b in range(local):
            to = b * n + g * some * per
            out[to : to + some * per, :] = moved[b * some * per : (b + 1) * some * per, :]


def middle_kernel(groups, at, got, w2, w3, send, *rest):
    shares, (mixed, d_down, act, d_pre, grads) = rest[:X_SIZE], rest[X_SIZE:]
    local, width, hidden = w2.shape
    mine = local // Z_LOW
    tokens = got.shape[2]
    rows = send.shape[1] // 2
    parts = hidden // width
    base = at[0] * mine
    collect(got, 0, local, mixed)
    collect(got, 1, local, d_down)
    for zl in range(Z_LOW):
        cols = pl.ds(zl * tokens, tokens)
        downs, d_mixeds = [], []
        for b in range(mine):
            held = pl.ds(b * width, width)
            h = dot(w2[base + b], mixed[held, cols], TN)
            squared = h * h
            half = 0.5 + 0.5 * jnp.tanh(h * (ROOT + (ROOT * CUBIC) * squared))
            acted = (h * half).astype(BF)
            gain = half + h * (half - half * half) * (2.0 * ROOT + (6.0 * ROOT * CUBIC) * squared)
            d_act = dot(w3[base + b], d_down[held, cols], NN)
            d_h = (d_act * gain).astype(BF)
            downs.append(dot(w3[base + b], acted, TN))
            d_mixeds.append(dot(w2[base + b], d_h, NN))
            act[b, :, cols] = acted
            d_pre[b, :, cols] = d_h
        send[zl * groups : (zl + 1) * groups, :rows, :] = stack(*downs).astype(BF)
        send[zl * groups : (zl + 1) * groups, rows:, :] = stack(*d_mixeds).astype(BF)
    for b in range(mine):
        held = pl.ds(b * width, width)
        second = dot(mixed[held, :], d_pre[b], NT).astype(BF)
        for j in range(parts):
            part = slice(j * width, (j + 1) * width)
            grads[b, part, :] = second[:, part]
        grads[mine + b] = dot(act[b], d_down[held, :], NT).astype(BF)
    for k in range(X_SIZE):
        shares[k][...] = grads[(at[1] + k) % X_SIZE]


def leave_kernel(got, x, dy, *rest):
    *shares, back, d_first, grads, wide_sum = rest
    acc = shares[0][...].astype(F32)
    for share in shares[1:]:
        acc = acc + share[...].astype(F32)
    wide_sum[...] = acc.astype(BF)
    parts, width, _ = grads.shape
    local = parts // 2
    collect_back(got, 0, local, back)
    collect_back(got, 1, local, d_first)
    for b in range(local):
        rows = pl.ds(b * width, width)
        grads[b] = dot(x[:, rows], d_first[rows, :], TT).astype(BF)
        grads[local + b] = dot(back[rows, :], dy[:, rows], NN).astype(BF)


def outputs_kernel(back, d_first, w1, w4, output, grad_tokens):
    local, width, _ = w1.shape
    for b in range(local):
        cols = pl.ds(b * width, width)
        output[:, cols] = dot(back[cols, :], w4[b], TN).astype(BF)
        grad_tokens[:, cols] = dot(d_first[cols, :], w1[b], TT).astype(BF)


def add_kernel(got, wide_sum, total):
    high = wide_sum.shape[0]
    total[:high, :] = wide_sum[...]
    acc = got[0].astype(F32)
    for k in range(1, got.shape[0]):
        acc = acc + got[k].astype(F32)
    total[high:, :] = acc.astype(BF)


def add_copy_kernel(scale, got, copies):
    acc = got[0].astype(F32)
    for k in range(1, got.shape[0]):
        acc = acc + got[k].astype(F32)
    total = (acc * scale).astype(BF)
    for k in range(copies.shape[0]):
        copies[k] = total


def unpack_kernel(got, first, second, third, fourth):
    local, width, hidden = second.shape
    parts = hidden // width
    mine = local // Z_LOW
    for b in range(local):
        k = b // mine * X_SIZE + b % mine
        for j in range(parts):
            part = slice(j * width, (j + 1) * width)
            second[b, :, part] = got[k, part, :]
        third[b] = got[k + mine, :hidden, :]
        first[b] = got[b, hidden:, :]
        fourth[b] = got[local + b, hidden:, :]


def exchange(value, axes):
    return lax.all_to_all(value, axes, split_axis=0, concat_axis=0, tiled=True)


def body(all_tokens, tokens, w_first, w_second, w_third, w_fourth, upstream):
    count, wide = tokens.shape
    local, width, hidden = w_second.shape
    groups = lax.axis_size("hidden")
    near, middle = ("zl", "x"), ("zl", "hidden")
    parts = Z_LOW * X_SIZE
    mine = local // Z_LOW
    scale = float(all_tokens) ** -0.5
    rows = 2 * local * mine * PAIR
    place = jnp.stack([lax.axis_index("zl"), lax.axis_index("x")]).astype(jnp.int32)
    entering = (tokens, w_first, upstream, w_fourth)
    (send,) = call(
        functools.partial(enter_kernel, groups),
        [shape(Z_LOW * groups, rows, count)],
        *entering,
        flops=4 * count * wide * width, vmem=60 << 20,
        in_specs=[pl.BlockSpec(memory_space=pltpu.HBM)] * 4,
        scratch_shapes=[pltpu.VMEM(a.shape, BF) for a in entering]
        + [pltpu.SemaphoreType.DMA((4,))],
    )
    got = exchange(send, middle)
    both = Z_LOW * count
    send, *shares = call(
        functools.partial(middle_kernel, groups),
        [shape(Z_LOW * groups, rows, count)] + [shape(hidden, width)] * X_SIZE,
        place, got, w_second, w_third,
        flops=12 * count * wide * hidden, transcendentals=count * local * hidden,
        in_specs=[pl.BlockSpec(memory_space=pltpu.SMEM)] + [pl.BlockSpec()] * 3,
        scratch_shapes=[pltpu.VMEM((mine * width, both), BF)] * 2
        + [pltpu.VMEM((mine, hidden, both), BF)] * 2
        + [pltpu.VMEM((X_SIZE, hidden, width), BF)],
    )
    got = exchange(send, middle)
    shares = [
        share if k == 0 else lax.ppermute(share, "x", [(i, (i + k) % X_SIZE) for i in range(X_SIZE)])
        for k, share in enumerate(shares)
    ]
    back, d_first, grads, wide_sum = call(
        leave_kernel,
        [
            shape(wide, count), shape(wide, count), shape(parts, width, width),
            shape(hidden, width),
        ],
        got, tokens, upstream, *shares,
        flops=8 * count * wide * width,
    )
    got = exchange(grads, near)
    output, grad_tokens = call(
        outputs_kernel, [shape(count, wide), shape(count, wide)],
        back, d_first, w_first, w_fourth,
        flops=4 * count * wide * width,
    )
    (total,) = call(
        add_kernel, [shape(hidden + width, width)], got, wide_sum, flops=4 * hidden * width
    )
    got = lax.all_gather(total, "far", axis=0, tiled=False)
    (copies,) = call(
        functools.partial(add_copy_kernel, scale),
        [shape(parts, hidden + width, width)], got, flops=got.size,
    )
    got = exchange(copies, near)
    first, second, third, fourth = call(
        unpack_kernel,
        [shape(*w.shape) for w in (w_first, w_second, w_third, w_fourth)],
        got,
    )
    return output, grad_tokens, first, second, third, fourth


def solution(mesh):
    seq, groups = mesh.shape["seq"], mesh.shape["hidden"]
    fine = Mesh(
        mesh.devices.reshape(seq // (Z_LOW * X_SIZE), Z_LOW, X_SIZE, groups),
        ("far", "zl", "x", "hidden"),
    )
    rows = P(("far", "zl", "x"), "hidden")
    weight = P("hidden", None, None)

    def run(tokens, w_first, w_second, w_third, w_fourth, upstream):
        return jax.shard_map(
            functools.partial(body, tokens.shape[0]),
            mesh=fine,
            in_specs=(rows, weight, weight, weight, weight, rows),
            out_specs=(rows, rows, weight, weight, weight, weight),
            check_vma=False,
        )(tokens, w_first, w_second, w_third, w_fourth, upstream)

    return run
```

```python
import functools

import jax
import jax.numpy as jnp
from jax import lax
from jax.experimental import pallas as pl
from jax.experimental.pallas import tpu as pltpu
from jax.sharding import Mesh, PartitionSpec as P

ROOT = 0.7978845608
CUBIC = 0.044715
BF = jnp.bfloat16
F32 = jnp.float32
PAIR = 2
Z_LOW = 2
X_SIZE = 4
NN = (((1,), (0,)), ((), ()))
NT = (((1,), (1,)), ((), ()))
TN = (((0,), (0,)), ((), ()))
TT = (((0,), (1,)), ((), ()))


def dot(a, b, dims):
    return lax.dot_general(a, b, dims, preferred_element_type=F32)


def call(kernel, outs, *args, flops=0, transcendentals=0, vmem=24 << 20, **more):
    moved = sum(a.size * a.dtype.itemsize for a in (*args, *outs))
    return pl.pallas_call(
        kernel,
        out_shape=outs,
        compiler_params=pltpu.CompilerParams(vmem_limit_bytes=vmem),
        cost_estimate=pl.CostEstimate(
            flops=int(flops), bytes_accessed=int(moved), transcendentals=int(transcendentals)
        ),
        **more,
    )(*args)


def shape(*dims, dtype=BF):
    return jax.ShapeDtypeStruct(dims, dtype)


def swap_units(tiles):
    row = lax.broadcasted_iota(jnp.int32, tiles[0].shape, 1)
    tiles = list(tiles)
    per = tiles[0].shape[1]
    for step in (len(tiles) // 2, len(tiles) // 4):
        shift = step * PAIR
        stay = (row // shift) % 2 == 0
        for k in range(len(tiles)):
            if k // step % 2 == 0:
                low, high = tiles[k], tiles[k + step]
                tiles[k] = jnp.where(stay, low, pltpu.roll(high, shift, 1))
                tiles[k + step] = jnp.where(stay, pltpu.roll(low, per - shift, 1), high)
    return tiles


def enter_kernel(groups, x_in, w1_in, dy_in, w4_in, send, x, w1, dy, w4, arrived):
    copies = [
        pltpu.make_async_copy(source, target, arrived.at[k])
        for k, (source, target) in enumerate(((x_in, x), (w1_in, w1), (dy_in, dy), (w4_in, w4)))
    ]
    for copy in copies:
        copy.start()
    local, width, _ = w1.shape
    tokens = x.shape[0]
    halves = []
    for k in range(2):
        copies[2 * k].wait()
        copies[2 * k + 1].wait()
        tiles = []
        for b in range(local):
            cols = pl.ds(b * width, width)
            z = dot(w1[b], x[:, cols], TT) if k == 0 else dot(w4[b], dy[:, cols], NT)
            tiles.append(z.reshape(groups, width // groups, tokens))
        halves.append(swap_units(tiles))
    for q in range(local):
        both = jnp.concatenate([halves[0][q], halves[1][q]], axis=1)
        send[q * groups : (q + 1) * groups] = both.astype(BF)


def middle_kernel(groups, at, got, w2, w3, send, own, other, mixed, d_down, act, d_pre, grads):
    _, width, hidden = w2.shape
    tokens = got.shape[2]
    per = width // groups
    parts = hidden // width
    zl, block = at[0], at[1]
    for s in range(X_SIZE):
        cols = pl.ds(s * tokens, tokens)
        members = slice(s * groups, (s + 1) * groups)
        taken = got[members].astype(F32)
        mixed[:, cols] = taken[:, :per, :].reshape(width, tokens).astype(BF)
        d_down[:, cols] = taken[:, per:, :].reshape(width, tokens).astype(BF)
        h = dot(w2[block], mixed[:, cols], TN)
        squared = h * h
        half = 0.5 + 0.5 * jnp.tanh(h * (ROOT + (ROOT * CUBIC) * squared))
        acted = (h * half).astype(BF)
        gain = half + h * (half - half * half) * (2.0 * ROOT + (6.0 * ROOT * CUBIC) * squared)
        d_h = (dot(w3[block], d_down[:, cols], NN) * gain).astype(BF)
        down = dot(w3[block], acted, TN).reshape(groups, per, tokens)
        d_mixed = dot(w2[block], d_h, NN).reshape(groups, per, tokens)
        send[members] = jnp.concatenate([down, d_mixed], axis=1).astype(BF)
        act[:, cols] = acted
        d_pre[:, cols] = d_h
    second = dot(mixed[...], d_pre[...], NT).astype(BF)
    for j in range(parts):
        part = slice(j * width, (j + 1) * width)
        grads[0, part, :] = second[:, part]
    grads[1] = dot(act[...], d_down[...], NT).astype(BF)
    own[...] = grads[zl]
    other[...] = grads[1 - zl]


def pair_kernel(own, other, total):
    total[...] = (own[...].astype(F32) + other[...].astype(F32)).astype(BF)


def leave_kernel(scale, got, x, dy, *rest):
    *shares, back, d_first, grads, wide_sum = rest
    acc = shares[0][...].astype(F32)
    for share in shares[1:]:
        acc = acc + share[...].astype(F32)
    wide_sum[...] = (acc * scale).astype(BF)
    parts, width, _ = grads.shape
    local = parts // 2
    count, rows, tokens = got.shape
    groups, per = count // X_SIZE, rows // 2
    taken = [got[s * groups : (s + 1) * groups].astype(F32) for s in range(X_SIZE)]
    for k, out in enumerate((back, d_first)):
        tiles = swap_units([t[:, k * per : (k + 1) * per, :] for t in taken])
        for b in range(local):
            out[b * width : (b + 1) * width, :] = tiles[b].reshape(width, tokens).astype(BF)
    for b in range(local):
        held = pl.ds(b * width, width)
        grads[b] = dot(x[:, held], d_first[held, :], TT).astype(BF)
        grads[local + b] = dot(back[held, :], dy[:, held], NN).astype(BF)


def outputs_kernel(back, d_first, w1, w4, output, grad_tokens):
    local, width, _ = w1.shape
    for b in range(local):
        cols = pl.ds(b * width, width)
        output[:, cols] = dot(back[cols, :], w4[b], TN).astype(BF)
        grad_tokens[:, cols] = dot(d_first[cols, :], w1[b], TT).astype(BF)


def add_kernel(got, copies):
    acc = got[0].astype(F32)
    for k in range(1, got.shape[0]):
        acc = acc + got[k].astype(F32)
    total = acc.astype(BF)
    for k in range(copies.shape[0]):
        copies[k] = total


def add_copy_kernel(scale, got, wide_sum, copies):
    high = wide_sum.shape[0]
    acc = got[0].astype(F32)
    for k in range(1, got.shape[0]):
        acc = acc + got[k].astype(F32)
    total = (acc * scale).astype(BF)
    for k in range(copies.shape[0]):
        copies[k, :high, :] = wide_sum[...]
        copies[k, high:, :] = total


def unpack_kernel(got, first, second, third, fourth):
    local, width, hidden = second.shape
    for b in range(local):
        for j in range(hidden // width):
            part = slice(j * width, (j + 1) * width)
            second[b, :, part] = got[b, part, :]
        third[b] = got[local + b, :hidden, :]
        first[b] = got[b, hidden:, :]
        fourth[b] = got[local + b, hidden:, :]


def exchange(value, axes):
    return lax.all_to_all(value, axes, split_axis=0, concat_axis=0, tiled=True)


def body(all_tokens, tokens, w_first, w_second, w_third, w_fourth, upstream):
    count, wide = tokens.shape
    local, width, hidden = w_second.shape
    groups = lax.axis_size("hidden")
    near, middle = ("zl", "x"), ("x", "hidden")
    parts = Z_LOW * X_SIZE
    scale = float(all_tokens) ** -0.5
    rows = 2 * local * PAIR
    place = jnp.stack([lax.axis_index("zl"), lax.axis_index("x")]).astype(jnp.int32)
    entering = (tokens, w_first, upstream, w_fourth)
    (send,) = call(
        functools.partial(enter_kernel, groups),
        [shape(X_SIZE * groups, rows, count)],
        *entering,
        flops=4 * count * wide * width, vmem=60 << 20,
        in_specs=[pl.BlockSpec(memory_space=pltpu.HBM)] * 4,
        scratch_shapes=[pltpu.VMEM(a.shape, BF) for a in entering]
        + [pltpu.SemaphoreType.DMA((4,))],
    )
    got = exchange(send, middle)
    every = X_SIZE * count
    send, own, other = call(
        functools.partial(middle_kernel, groups),
        [shape(X_SIZE * groups, rows, count)] + [shape(hidden, width)] * 2,
        place, got, w_second, w_third,
        flops=12 * count * wide * hidden, transcendentals=count * local * hidden,
        in_specs=[pl.BlockSpec(memory_space=pltpu.SMEM)] + [pl.BlockSpec()] * 3,
        scratch_shapes=[pltpu.VMEM((width, every), BF)] * 2
        + [pltpu.VMEM((hidden, every), BF)] * 2
        + [pltpu.VMEM((2, hidden, width), BF)],
    )
    got = exchange(send, middle)
    far = lax.axis_size("far")
    other = lax.ppermute(other, "zl", [(0, 1), (1, 0)])
    (wide_sum,) = call(pair_kernel, [shape(hidden, width)], own, other, flops=hidden * width)
    shares = [wide_sum] + [
        lax.ppermute(wide_sum, "far", [(i, (i + k) % far) for i in range(far)])
        for k in range(1, far)
    ]
    back, d_first, grads, wide_sum = call(
        functools.partial(leave_kernel, scale),
        [
            shape(wide, count), shape(wide, count), shape(parts, width, width),
            shape(hidden, width),
        ],
        got, tokens, upstream, *shares,
        flops=8 * count * wide * width,
    )
    got = exchange(grads, near)
    output, grad_tokens = call(
        outputs_kernel, [shape(count, wide), shape(count, wide)],
        back, d_first, w_first, w_fourth,
        flops=4 * count * wide * width,
    )
    (copies,) = call(add_kernel, [shape(far, width, width)], got, flops=got.size)
    got = exchange(copies, "far")
    (copies,) = call(
        functools.partial(add_copy_kernel, scale),
        [shape(parts, hidden + width, width)], got, wide_sum, flops=got.size,
    )
    got = exchange(copies, near)
    first, second, third, fourth = call(
        unpack_kernel,
        [shape(*w.shape) for w in (w_first, w_second, w_third, w_fourth)],
        got,
    )
    return output, grad_tokens, first, second, third, fourth


def solution(mesh):
    seq, groups = mesh.shape["seq"], mesh.shape["hidden"]
    fine = Mesh(
        mesh.devices.reshape(seq // (Z_LOW * X_SIZE), Z_LOW, X_SIZE, groups),
        ("far", "zl", "x", "hidden"),
    )
    rows = P(("far", "zl", "x"), "hidden")
    weight = P("hidden", None, None)

    def run(tokens, w_first, w_second, w_third, w_fourth, upstream):
        return jax.shard_map(
            functools.partial(body, tokens.shape[0]),
            mesh=fine,
            in_specs=(rows, weight, weight, weight, weight, rows),
            out_specs=(rows, rows, weight, weight, weight, weight),
            check_vma=False,
        )(tokens, w_first, w_second, w_third, w_fourth, upstream)

    return run
```

```python
import functools

import jax
import jax.numpy as jnp
from jax import lax
from jax.experimental import pallas as pl
from jax.experimental.pallas import tpu as pltpu
from jax.sharding import Mesh, PartitionSpec as P

ROOT = 0.7978845608
CUBIC = 0.044715
BF = jnp.bfloat16
F32 = jnp.float32
PAIR = 2
Z_LOW = 2
X_SIZE = 4
NN = (((1,), (0,)), ((), ()))
NT = (((1,), (1,)), ((), ()))
TN = (((0,), (0,)), ((), ()))
TT = (((0,), (1,)), ((), ()))


def dot(a, b, dims):
    return lax.dot_general(a, b, dims, preferred_element_type=F32)


def call(kernel, outs, *args, flops=0, transcendentals=0, vmem=24 << 20, **more):
    moved = sum(a.size * a.dtype.itemsize for a in (*args, *outs))
    return pl.pallas_call(
        kernel,
        out_shape=outs,
        compiler_params=pltpu.CompilerParams(vmem_limit_bytes=vmem),
        cost_estimate=pl.CostEstimate(
            flops=int(flops), bytes_accessed=int(moved), transcendentals=int(transcendentals)
        ),
        **more,
    )(*args)


def shape(*dims, dtype=BF):
    return jax.ShapeDtypeStruct(dims, dtype)


def stack(low, high):
    width, tokens = low.shape
    per = 2 * PAIR * Z_LOW
    split = (width // per, per, tokens)
    return jnp.concatenate([low.reshape(split), high.reshape(split)], axis=1)


def enter_kernel(groups, x_in, w1_in, dy_in, w4_in, send, x, w1, dy, w4, arrived):
    copies = [
        pltpu.make_async_copy(source, target, arrived.at[k])
        for k, (source, target) in enumerate(((x_in, x), (w1_in, w1), (dy_in, dy), (w4_in, w4)))
    ]
    for copy in copies:
        copy.start()
    local, width, _ = w1.shape
    tokens = x.shape[0]
    per = width // groups
    rows = local * per // Z_LOW
    first_half = lax.broadcasted_iota(jnp.int32, (groups, per, tokens), 1) < per // 2
    for k in range(2):
        copies[2 * k].wait()
        copies[2 * k + 1].wait()
        to_zl = [[], []]
        for pair in range(local // 2):
            both = []
            for b in (2 * pair, 2 * pair + 1):
                cols = pl.ds(b * width, width)
                if k == 0:
                    z = dot(w1[b], x[:, cols], TT)
                else:
                    z = dot(w4[b], dy[:, cols], NT)
                both.append(z.reshape(groups, per, tokens))
            low, high = both
            to_zl[0].append(jnp.where(first_half, low, pltpu.roll(high, per // 2, 1)))
            to_zl[1].append(jnp.where(first_half, pltpu.roll(low, per // 2, 1), high))
        for zl in range(Z_LOW):
            filled = jnp.concatenate(to_zl[zl], axis=1).astype(BF)
            send[zl * groups : (zl + 1) * groups, k * rows : (k + 1) * rows, :] = filled


def one_hot(source):
    n = source.shape[0]
    return (lax.broadcasted_iota(jnp.int32, (n, n), 1) == source).astype(F32).astype(BF)


def collect(got, k, theirs, out):
    count, rows, tokens = got.shape
    groups, held = count // Z_LOW, rows // 2
    mine = held // (theirs * PAIR)
    n = out.shape[0] // mine
    some = n // held
    per = theirs * PAIR
    r = lax.broadcasted_iota(jnp.int32, (n, 1), 0)
    own, group = r // (some * per), (r // per) % some
    their, one = (r // PAIR) % theirs, r % PAIR
    order = one_hot(group * held + their * (mine * PAIR) + own * PAIR + one)
    for zl in range(Z_LOW):
        for g in range(groups // some):
            at = zl * groups + g * some
            taken = got[at : at + some, k * held : (k + 1) * held, :].reshape(n, tokens)
            moved = dot(order, taken, NN).astype(BF)
            for b in range(mine):
                to = b * n + g * some * per
                out[to : to + some * per, zl * tokens : (zl + 1) * tokens] = moved[
                    b * some * per : (b + 1) * some * per, :
                ]


def collect_back(got, k, local, out):
    count, rows, tokens = got.shape
    groups, held = count // Z_LOW, rows // 2
    theirs = held // (local * PAIR)
    n = out.shape[0] // local
    some = n // (Z_LOW * held)
    per = Z_LOW * theirs * PAIR
    r = lax.broadcasted_iota(jnp.int32, (n, 1), 0)
    own, group = r // (some * per), (r // per) % some
    zl, their, one = (r // (theirs * PAIR)) % Z_LOW, (r // PAIR) % theirs, r % PAIR
    order = one_hot((zl * some + group) * held + their * (local * PAIR) + own * PAIR + one)
    for g in range(groups // some):
        taken = jnp.concatenate(
            [
                got[z * groups + g * some : z * groups + (g + 1) * some, k * held : (k + 1) * held, :]
                .reshape(some * held, tokens)
                for z in range(Z_LOW)
            ],
            axis=0,
        )
        moved = dot(order, taken, NN).astype(BF)
        for b in range(local):
            to = b * n + g * some * per
            out[to : to + some * per, :] = moved[b * some * per : (b + 1) * some * per, :]


def middle_kernel(groups, at, got, w2, w3, send, *rest):
    shares, (mixed, d_down, act, d_pre, grads) = rest[:X_SIZE], rest[X_SIZE:]
    local, width, hidden = w2.shape
    mine = local // Z_LOW
    tokens = got.shape[2]
    rows = send.shape[1] // 2
    parts = hidden // width
    base = at[0] * mine
    collect(got, 0, local, mixed)
    collect(got, 1, local, d_down)
    downs, d_mixeds = [], []
    for b in range(mine):
        held = pl.ds(b * width, width)
        h = dot(w2[base + b], mixed[held, :], TN)
        squared = h * h
        half = 0.5 + 0.5 * jnp.tanh(h * (ROOT + (ROOT * CUBIC) * squared))
        act[b] = (h * half).astype(BF)
        gain = half + h * (half - half * half) * (2.0 * ROOT + (6.0 * ROOT * CUBIC) * squared)
        d_pre[b] = (dot(w3[base + b], d_down[held, :], NN) * gain).astype(BF)
        downs.append(dot(w3[base + b], act[b], TN))
        d_mixeds.append(dot(w2[base + b], d_pre[b], NN))
        second = dot(mixed[held, :], d_pre[b], NT).astype(BF)
        for j in range(parts):
            part = slice(j * width, (j + 1) * width)
            grads[b, part, :] = second[:, part]
        grads[mine + b] = dot(act[b], d_down[held, :], NT).astype(BF)
    for zl in range(Z_LOW):
        cols = slice(zl * tokens, (zl + 1) * tokens)
        members = slice(zl * groups, (zl + 1) * groups)
        send[members, :rows, :] = stack(*[z[:, cols] for z in downs]).astype(BF)
        send[members, rows:, :] = stack(*[z[:, cols] for z in d_mixeds]).astype(BF)
    for k in range(X_SIZE):
        shares[k][...] = grads[(at[1] + k) % X_SIZE]


def leave_kernel(got, x, dy, *rest):
    *shares, back, d_first, grads, wide_sum = rest
    acc = shares[0][...].astype(F32)
    for share in shares[1:]:
        acc = acc + share[...].astype(F32)
    wide_sum[...] = acc.astype(BF)
    parts, width, _ = grads.shape
    local = parts // 2
    collect_back(got, 0, local, back)
    collect_back(got, 1, local, d_first)
    for b in range(local):
        rows = pl.ds(b * width, width)
        grads[b] = dot(x[:, rows], d_first[rows, :], TT).astype(BF)
        grads[local + b] = dot(back[rows, :], dy[:, rows], NN).astype(BF)


def outputs_kernel(back, d_first, w1, w4, output, grad_tokens):
    local, width, _ = w1.shape
    for b in range(local):
        cols = pl.ds(b * width, width)
        output[:, cols] = dot(back[cols, :], w4[b], TN).astype(BF)
        grad_tokens[:, cols] = dot(d_first[cols, :], w1[b], TT).astype(BF)


def add_kernel(got, wide_sum, total):
    high = wide_sum.shape[0]
    total[:high, :] = wide_sum[...]
    acc = got[0].astype(F32)
    for k in range(1, got.shape[0]):
        acc = acc + got[k].astype(F32)
    total[high:, :] = acc.astype(BF)


def add_copy_kernel(scale, got, copies):
    acc = got[0].astype(F32)
    for k in range(1, got.shape[0]):
        acc = acc + got[k].astype(F32)
    total = (acc * scale).astype(BF)
    for k in range(copies.shape[0]):
        copies[k] = total


def unpack_kernel(got, first, second, third, fourth):
    local, width, hidden = second.shape
    parts = hidden // width
    mine = local // Z_LOW
    for b in range(local):
        k = b // mine * X_SIZE + b % mine
        for j in range(parts):
            part = slice(j * width, (j + 1) * width)
            second[b, :, part] = got[k, part, :]
        third[b] = got[k + mine, :hidden, :]
        first[b] = got[b, hidden:, :]
        fourth[b] = got[local + b, hidden:, :]


def exchange(value, axes):
    return lax.all_to_all(value, axes, split_axis=0, concat_axis=0, tiled=True)


def body(all_tokens, tokens, w_first, w_second, w_third, w_fourth, upstream):
    count, wide = tokens.shape
    local, width, hidden = w_second.shape
    groups = lax.axis_size("hidden")
    near, middle = ("zl", "x"), ("zl", "hidden")
    parts = Z_LOW * X_SIZE
    mine = local // Z_LOW
    scale = float(all_tokens) ** -0.5
    rows = 2 * local * mine * PAIR
    place = jnp.stack([lax.axis_index("zl"), lax.axis_index("x")]).astype(jnp.int32)
    entering = (tokens, w_first, upstream, w_fourth)
    (send,) = call(
        functools.partial(enter_kernel, groups),
        [shape(Z_LOW * groups, rows, count)],
        *entering,
        flops=4 * count * wide * width, vmem=60 << 20,
        in_specs=[pl.BlockSpec(memory_space=pltpu.HBM)] * 4,
        scratch_shapes=[pltpu.VMEM(a.shape, BF) for a in entering]
        + [pltpu.SemaphoreType.DMA((4,))],
    )
    got = exchange(send, middle)
    both = Z_LOW * count
    send, *shares = call(
        functools.partial(middle_kernel, groups),
        [shape(Z_LOW * groups, rows, count)] + [shape(hidden, width)] * X_SIZE,
        place, got, w_second, w_third,
        flops=12 * count * wide * hidden, transcendentals=count * local * hidden,
        in_specs=[pl.BlockSpec(memory_space=pltpu.SMEM)] + [pl.BlockSpec()] * 3,
        scratch_shapes=[pltpu.VMEM((mine * width, both), BF)] * 2
        + [pltpu.VMEM((mine, hidden, both), BF)] * 2
        + [pltpu.VMEM((X_SIZE, hidden, width), BF)],
    )
    got = exchange(send, middle)
    shares = [
        share if k == 0 else lax.ppermute(share, "x", [(i, (i + k) % X_SIZE) for i in range(X_SIZE)])
        for k, share in enumerate(shares)
    ]
    back, d_first, grads, wide_sum = call(
        leave_kernel,
        [
            shape(wide, count), shape(wide, count), shape(parts, width, width),
            shape(hidden, width),
        ],
        got, tokens, upstream, *shares,
        flops=8 * count * wide * width,
    )
    got = exchange(grads, near)
    output, grad_tokens = call(
        outputs_kernel, [shape(count, wide), shape(count, wide)],
        back, d_first, w_first, w_fourth,
        flops=4 * count * wide * width,
    )
    got, output, grad_tokens = lax.optimization_barrier((got, output, grad_tokens))
    (total,) = call(
        add_kernel, [shape(hidden + width, width)], got, wide_sum, flops=4 * hidden * width
    )
    got = lax.all_gather(total, "far", axis=0, tiled=False)
    (copies,) = call(
        functools.partial(add_copy_kernel, scale),
        [shape(parts, hidden + width, width)], got, flops=got.size,
    )
    got = exchange(copies, near)
    first, second, third, fourth = call(
        unpack_kernel,
        [shape(*w.shape) for w in (w_first, w_second, w_third, w_fourth)],
        got,
    )
    return output, grad_tokens, first, second, third, fourth


def solution(mesh):
    seq, groups = mesh.shape["seq"], mesh.shape["hidden"]
    fine = Mesh(
        mesh.devices.reshape(seq // (Z_LOW * X_SIZE), Z_LOW, X_SIZE, groups),
        ("far", "zl", "x", "hidden"),
    )
    rows = P(("far", "zl", "x"), "hidden")
    weight = P("hidden", None, None)

    def run(tokens, w_first, w_second, w_third, w_fourth, upstream):
        return jax.shard_map(
            functools.partial(body, tokens.shape[0]),
            mesh=fine,
            in_specs=(rows, weight, weight, weight, weight, rows),
            out_specs=(rows, rows, weight, weight, weight, weight),
            check_vma=False,
        )(tokens, w_first, w_second, w_third, w_fourth, upstream)

    return run
```

```python
import functools

import jax
import jax.numpy as jnp
from jax import lax
from jax.experimental import pallas as pl
from jax.experimental.pallas import tpu as pltpu
from jax.sharding import Mesh, PartitionSpec as P

ROOT = 0.7978845608
CUBIC = 0.044715
BF = jnp.bfloat16
F32 = jnp.float32
PAIR = 2
Z_LOW = 2
X_SIZE = 4
NN = (((1,), (0,)), ((), ()))
NT = (((1,), (1,)), ((), ()))
TN = (((0,), (0,)), ((), ()))
TT = (((0,), (1,)), ((), ()))


def dot(a, b, dims):
    return lax.dot_general(a, b, dims, preferred_element_type=F32)


def call(kernel, outs, *args, flops=0, transcendentals=0, vmem=24 << 20, **more):
    moved = sum(a.size * a.dtype.itemsize for a in (*args, *outs))
    return pl.pallas_call(
        kernel,
        out_shape=outs,
        compiler_params=pltpu.CompilerParams(vmem_limit_bytes=vmem),
        cost_estimate=pl.CostEstimate(
            flops=int(flops), bytes_accessed=int(moved), transcendentals=int(transcendentals)
        ),
        **more,
    )(*args)


def shape(*dims, dtype=BF):
    return jax.ShapeDtypeStruct(dims, dtype)


def stack(low, high):
    width, tokens = low.shape
    per = 2 * PAIR * Z_LOW
    split = (width // per, per, tokens)
    return jnp.concatenate([low.reshape(split), high.reshape(split)], axis=1)


def enter_kernel(groups, x_in, w1_in, dy_in, w4_in, send, x, w1, dy, w4, arrived):
    copies = [
        pltpu.make_async_copy(source, target, arrived.at[k])
        for k, (source, target) in enumerate(((x_in, x), (w1_in, w1), (dy_in, dy), (w4_in, w4)))
    ]
    for copy in copies:
        copy.start()
    local, width, _ = w1.shape
    tokens = x.shape[0]
    per = width // groups
    rows = local * per // Z_LOW
    first_half = lax.broadcasted_iota(jnp.int32, (groups, per, tokens), 1) < per // 2
    for k in range(2):
        copies[2 * k].wait()
        copies[2 * k + 1].wait()
        to_zl = [[], []]
        for pair in range(local // 2):
            both = []
            for b in (2 * pair, 2 * pair + 1):
                cols = pl.ds(b * width, width)
                if k == 0:
                    z = dot(w1[b], x[:, cols], TT)
                else:
                    z = dot(w4[b], dy[:, cols], NT)
                both.append(z.reshape(groups, per, tokens))
            low, high = both
            to_zl[0].append(jnp.where(first_half, low, pltpu.roll(high, per // 2, 1)))
            to_zl[1].append(jnp.where(first_half, pltpu.roll(low, per // 2, 1), high))
        for zl in range(Z_LOW):
            filled = jnp.concatenate(to_zl[zl], axis=1).astype(BF)
            send[zl * groups : (zl + 1) * groups, k * rows : (k + 1) * rows, :] = filled


def one_hot(source):
    n = source.shape[0]
    return (lax.broadcasted_iota(jnp.int32, (n, n), 1) == source).astype(F32).astype(BF)


def collect(got, k, theirs, out):
    count, rows, tokens = got.shape
    groups, held = count // Z_LOW, rows // 2
    mine = held // (theirs * PAIR)
    n = out.shape[0] // mine
    some = n // held
    per = theirs * PAIR
    r = lax.broadcasted_iota(jnp.int32, (n, 1), 0)
    own, group = r // (some * per), (r // per) % some
    their, one = (r // PAIR) % theirs, r % PAIR
    order = one_hot(group * held + their * (mine * PAIR) + own * PAIR + one)
    for zl in range(Z_LOW):
        for g in range(groups // some):
            at = zl * groups + g * some
            taken = got[at : at + some, k * held : (k + 1) * held, :].reshape(n, tokens)
            moved = dot(order, taken, NN).astype(BF)
            for b in range(mine):
                to = b * n + g * some * per
                out[to : to + some * per, zl * tokens : (zl + 1) * tokens] = moved[
                    b * some * per : (b + 1) * some * per, :
                ]


def collect_back(got, k, local, out):
    count, rows, tokens = got.shape
    groups, held = count // Z_LOW, rows // 2
    theirs = held // (local * PAIR)
    n = out.shape[0] // local
    some = n // (Z_LOW * held)
    per = Z_LOW * theirs * PAIR
    r = lax.broadcasted_iota(jnp.int32, (n, 1), 0)
    own, group = r // (some * per), (r // per) % some
    zl, their, one = (r // (theirs * PAIR)) % Z_LOW, (r // PAIR) % theirs, r % PAIR
    order = one_hot((zl * some + group) * held + their * (local * PAIR) + own * PAIR + one)
    for g in range(groups // some):
        taken = jnp.concatenate(
            [
                got[z * groups + g * some : z * groups + (g + 1) * some, k * held : (k + 1) * held, :]
                .reshape(some * held, tokens)
                for z in range(Z_LOW)
            ],
            axis=0,
        )
        moved = dot(order, taken, NN).astype(BF)
        for b in range(local):
            to = b * n + g * some * per
            out[to : to + some * per, :] = moved[b * some * per : (b + 1) * some * per, :]


def middle_kernel(groups, at, got, w2, w3, send, *rest):
    shares, (mixed, d_down, act, d_pre, grads, ready, left) = rest[:X_SIZE], rest[X_SIZE:]
    local, width, hidden = w2.shape
    mine = local // Z_LOW
    tokens = got.shape[2]
    rows = send.shape[1] // 2
    parts = hidden // width
    base = at[0] * mine
    collect(got, 0, local, mixed)
    collect(got, 1, local, d_down)
    for b in range(mine):
        held = pl.ds(b * width, width)
        h = dot(w2[base + b], mixed[held, :], TN)
        squared = h * h
        half = 0.5 + 0.5 * jnp.tanh(h * (ROOT + (ROOT * CUBIC) * squared))
        act[b] = (h * half).astype(BF)
        gain = half + h * (half - half * half) * (2.0 * ROOT + (6.0 * ROOT * CUBIC) * squared)
        d_pre[b] = (dot(w3[base + b], d_down[held, :], NN) * gain).astype(BF)
    leaving = []
    for k, (w, value, dims) in enumerate(((w3, act, TN), (w2, d_pre, NN))):
        results = [dot(w[base + b], value[b], dims) for b in range(mine)]
        part = slice(k * rows, (k + 1) * rows)
        for zl in range(Z_LOW):
            cols = slice(zl * tokens, (zl + 1) * tokens)
            members = slice(zl * groups, (zl + 1) * groups)
            ready[members, part, :] = stack(*[z[:, cols] for z in results]).astype(BF)
        part = pl.ds(k * rows, rows)
        copy = pltpu.make_async_copy(ready.at[:, part, :], send.at[:, part, :], left.at[k])
        copy.start()
        leaving.append(copy)
    for b in range(mine):
        held = pl.ds(b * width, width)
        second = dot(mixed[held, :], d_pre[b], NT).astype(BF)
        for j in range(parts):
            part = slice(j * width, (j + 1) * width)
            grads[b, part, :] = second[:, part]
        grads[mine + b] = dot(act[b], d_down[held, :], NT).astype(BF)
    for k in range(X_SIZE):
        shares[k][...] = grads[(at[1] + k) % X_SIZE]
    for copy in leaving:
        copy.wait()


def leave_kernel(got, x, dy, *rest):
    *shares, back, d_first, grads, wide_sum, ready, left = rest
    parts, width, _ = ready.shape
    local = parts // 2
    leaving = []

    def leave(k, value):
        ready[k] = value.astype(BF)
        copy = pltpu.make_async_copy(ready.at[k], grads.at[k], left.at[k])
        copy.start()
        leaving.append(copy)

    collect_back(got, 0, local, back)
    for b in range(local):
        rows = pl.ds(b * width, width)
        leave(local + b, dot(back[rows, :], dy[:, rows], NN))
    collect_back(got, 1, local, d_first)
    for b in range(local):
        rows = pl.ds(b * width, width)
        leave(b, dot(x[:, rows], d_first[rows, :], TT))
    acc = shares[0][...].astype(F32)
    for share in shares[1:]:
        acc = acc + share[...].astype(F32)
    wide_sum[...] = acc.astype(BF)
    for copy in leaving:
        copy.wait()


def outputs_kernel(back, d_first, w1, w4, output, grad_tokens):
    local, width, _ = w1.shape
    for b in range(local):
        cols = pl.ds(b * width, width)
        output[:, cols] = dot(back[cols, :], w4[b], TN).astype(BF)
        grad_tokens[:, cols] = dot(d_first[cols, :], w1[b], TT).astype(BF)


def add_kernel(got, wide_sum, total):
    high = wide_sum.shape[0]
    total[:high, :] = wide_sum[...]
    acc = got[0].astype(F32)
    for k in range(1, got.shape[0]):
        acc = acc + got[k].astype(F32)
    total[high:, :] = acc.astype(BF)


def add_copy_kernel(scale, got, copies):
    acc = got[0].astype(F32)
    for k in range(1, got.shape[0]):
        acc = acc + got[k].astype(F32)
    total = (acc * scale).astype(BF)
    for k in range(copies.shape[0]):
        copies[k] = total


def unpack_kernel(got, first, second, third, fourth):
    local, width, hidden = second.shape
    parts = hidden // width
    mine = local // Z_LOW
    for b in range(local):
        k = b // mine * X_SIZE + b % mine
        for j in range(parts):
            part = slice(j * width, (j + 1) * width)
            second[b, :, part] = got[k, part, :]
        third[b] = got[k + mine, :hidden, :]
        first[b] = got[b, hidden:, :]
        fourth[b] = got[local + b, hidden:, :]


def exchange(value, axes):
    return lax.all_to_all(value, axes, split_axis=0, concat_axis=0, tiled=True)


def body(all_tokens, tokens, w_first, w_second, w_third, w_fourth, upstream):
    count, wide = tokens.shape
    local, width, hidden = w_second.shape
    groups = lax.axis_size("hidden")
    near, middle = ("zl", "x"), ("zl", "hidden")
    parts = Z_LOW * X_SIZE
    mine = local // Z_LOW
    scale = float(all_tokens) ** -0.5
    rows = 2 * local * mine * PAIR
    place = jnp.stack([lax.axis_index("zl"), lax.axis_index("x")]).astype(jnp.int32)
    entering = (tokens, w_first, upstream, w_fourth)
    (send,) = call(
        functools.partial(enter_kernel, groups),
        [shape(Z_LOW * groups, rows, count)],
        *entering,
        flops=4 * count * wide * width, vmem=60 << 20,
        in_specs=[pl.BlockSpec(memory_space=pltpu.HBM)] * 4,
        scratch_shapes=[pltpu.VMEM(a.shape, BF) for a in entering]
        + [pltpu.SemaphoreType.DMA((4,))],
    )
    got = exchange(send, middle)
    both = Z_LOW * count
    send, *shares = call(
        functools.partial(middle_kernel, groups),
        [shape(Z_LOW * groups, rows, count)] + [shape(hidden, width)] * X_SIZE,
        place, got, w_second, w_third,
        flops=12 * count * wide * hidden, transcendentals=count * local * hidden,
        in_specs=[pl.BlockSpec(memory_space=pltpu.SMEM)] + [pl.BlockSpec()] * 3,
        scratch_shapes=[pltpu.VMEM((mine * width, both), BF)] * 2
        + [pltpu.VMEM((mine, hidden, both), BF)] * 2
        + [pltpu.VMEM((X_SIZE, hidden, width), BF), pltpu.VMEM(got.shape, BF)]
        + [pltpu.SemaphoreType.DMA((2,))],
        out_specs=[pl.BlockSpec(memory_space=pl.ANY)] + [pl.BlockSpec()] * X_SIZE,
    )
    got = exchange(send, middle)
    shares = [
        share if k == 0 else lax.ppermute(share, "x", [(i, (i + k) % X_SIZE) for i in range(X_SIZE)])
        for k, share in enumerate(shares)
    ]
    back, d_first, grads, wide_sum = call(
        leave_kernel,
        [
            shape(wide, count), shape(wide, count), shape(parts, width, width),
            shape(hidden, width),
        ],
        got, tokens, upstream, *shares,
        flops=8 * count * wide * width,
        out_specs=[
            pl.BlockSpec(), pl.BlockSpec(), pl.BlockSpec(memory_space=pl.ANY), pl.BlockSpec(),
        ],
        scratch_shapes=[
            pltpu.VMEM((parts, width, width), BF), pltpu.SemaphoreType.DMA((parts,)),
        ],
    )
    got = exchange(grads, near)
    output, grad_tokens = call(
        outputs_kernel, [shape(count, wide), shape(count, wide)],
        back, d_first, w_first, w_fourth,
        flops=4 * count * wide * width,
    )
    got, output, grad_tokens = lax.optimization_barrier((got, output, grad_tokens))
    (total,) = call(
        add_kernel, [shape(hidden + width, width)], got, wide_sum, flops=4 * hidden * width
    )
    got = lax.all_gather(total, "far", axis=0, tiled=False)
    (copies,) = call(
        functools.partial(add_copy_kernel, scale),
        [shape(parts, hidden + width, width)], got, flops=got.size,
    )
    got = exchange(copies, near)
    first, second, third, fourth = call(
        unpack_kernel,
        [shape(*w.shape) for w in (w_first, w_second, w_third, w_fourth)],
        got,
    )
    return output, grad_tokens, first, second, third, fourth


def solution(mesh):
    seq, groups = mesh.shape["seq"], mesh.shape["hidden"]
    fine = Mesh(
        mesh.devices.reshape(seq // (Z_LOW * X_SIZE), Z_LOW, X_SIZE, groups),
        ("far", "zl", "x", "hidden"),
    )
    rows = P(("far", "zl", "x"), "hidden")
    weight = P("hidden", None, None)

    def run(tokens, w_first, w_second, w_third, w_fourth, upstream):
        return jax.shard_map(
            functools.partial(body, tokens.shape[0]),
            mesh=fine,
            in_specs=(rows, weight, weight, weight, weight, rows),
            out_specs=(rows, rows, weight, weight, weight, weight),
            check_vma=False,
        )(tokens, w_first, w_second, w_third, w_fourth, upstream)

    return run
```

```python
import functools

import jax
import jax.numpy as jnp
from jax import lax
from jax.experimental import pallas as pl
from jax.experimental.pallas import tpu as pltpu
from jax.sharding import Mesh, PartitionSpec as P

ROOT = 0.7978845608
CUBIC = 0.044715
BF = jnp.bfloat16
F32 = jnp.float32
PAIR = 2
Z_LOW = 2
X_SIZE = 4
NN = (((1,), (0,)), ((), ()))
NT = (((1,), (1,)), ((), ()))
TN = (((0,), (0,)), ((), ()))
TT = (((0,), (1,)), ((), ()))


def dot(a, b, dims):
    return lax.dot_general(a, b, dims, preferred_element_type=F32)


def call(kernel, outs, *args, flops=0, transcendentals=0, vmem=24 << 20, **more):
    moved = sum(a.size * a.dtype.itemsize for a in (*args, *outs))
    return pl.pallas_call(
        kernel,
        out_shape=outs,
        compiler_params=pltpu.CompilerParams(vmem_limit_bytes=vmem),
        cost_estimate=pl.CostEstimate(
            flops=int(flops), bytes_accessed=int(moved), transcendentals=int(transcendentals)
        ),
        **more,
    )(*args)


def shape(*dims, dtype=BF):
    return jax.ShapeDtypeStruct(dims, dtype)


def stack(low, high):
    width, tokens = low.shape
    per = 2 * PAIR * Z_LOW
    split = (width // per, per, tokens)
    return jnp.concatenate([low.reshape(split), high.reshape(split)], axis=1)


def enter_kernel(groups, x_in, w1_in, dy_in, w4_in, send, x, w1, dy, w4, arrived):
    copies = [
        pltpu.make_async_copy(source, target, arrived.at[k])
        for k, (source, target) in enumerate(((x_in, x), (w1_in, w1), (dy_in, dy), (w4_in, w4)))
    ]
    for copy in copies:
        copy.start()
    local, width, _ = w1.shape
    tokens = x.shape[0]
    per = width // groups
    rows = local * per // Z_LOW
    first_half = lax.broadcasted_iota(jnp.int32, (groups, per, tokens), 1) < per // 2
    for k in range(2):
        copies[2 * k].wait()
        copies[2 * k + 1].wait()
        to_zl = [[], []]
        for pair in range(local // 2):
            both = []
            for b in (2 * pair, 2 * pair + 1):
                cols = pl.ds(b * width, width)
                if k == 0:
                    z = dot(w1[b], x[:, cols], TT)
                else:
                    z = dot(w4[b], dy[:, cols], NT)
                both.append(z.reshape(groups, per, tokens))
            low, high = both
            to_zl[0].append(jnp.where(first_half, low, pltpu.roll(high, per // 2, 1)))
            to_zl[1].append(jnp.where(first_half, pltpu.roll(low, per // 2, 1), high))
        for zl in range(Z_LOW):
            filled = jnp.concatenate(to_zl[zl], axis=1).astype(BF)
            send[zl * groups : (zl + 1) * groups, k * rows : (k + 1) * rows, :] = filled


def one_hot(source):
    n = source.shape[0]
    return (lax.broadcasted_iota(jnp.int32, (n, n), 1) == source).astype(F32).astype(BF)


def collect(got, k, theirs, out):
    count, rows, tokens = got.shape
    groups, held = count // Z_LOW, rows // 2
    mine = held // (theirs * PAIR)
    n = out.shape[0] // mine
    some = n // held
    per = theirs * PAIR
    r = lax.broadcasted_iota(jnp.int32, (n, 1), 0)
    own, group = r // (some * per), (r // per) % some
    their, one = (r // PAIR) % theirs, r % PAIR
    order = one_hot(group * held + their * (mine * PAIR) + own * PAIR + one)
    for zl in range(Z_LOW):
        for g in range(groups // some):
            at = zl * groups + g * some
            taken = got[at : at + some, k * held : (k + 1) * held, :].reshape(n, tokens)
            moved = dot(order, taken, NN).astype(BF)
            for b in range(mine):
                to = b * n + g * some * per
                out[to : to + some * per, zl * tokens : (zl + 1) * tokens] = moved[
                    b * some * per : (b + 1) * some * per, :
                ]


def collect_back(got, k, local, out):
    count, rows, tokens = got.shape
    groups, held = count // Z_LOW, rows // 2
    theirs = held // (local * PAIR)
    n = out.shape[0] // local
    some = n // (Z_LOW * held)
    per = Z_LOW * theirs * PAIR
    r = lax.broadcasted_iota(jnp.int32, (n, 1), 0)
    own, group = r // (some * per), (r // per) % some
    zl, their, one = (r // (theirs * PAIR)) % Z_LOW, (r // PAIR) % theirs, r % PAIR
    order = one_hot((zl * some + group) * held + their * (local * PAIR) + own * PAIR + one)
    for g in range(groups // some):
        taken = jnp.concatenate(
            [
                got[z * groups + g * some : z * groups + (g + 1) * some, k * held : (k + 1) * held, :]
                .reshape(some * held, tokens)
                for z in range(Z_LOW)
            ],
            axis=0,
        )
        moved = dot(order, taken, NN).astype(BF)
        for b in range(local):
            to = b * n + g * some * per
            out[to : to + some * per, :] = moved[b * some * per : (b + 1) * some * per, :]


def middle_kernel(groups, got, w2, w3, send, *rest):
    shares, (mixed, d_down, act, d_pre, grads, ready, left) = rest[:X_SIZE], rest[X_SIZE:]
    local, width, hidden = w2.shape
    mine = local // Z_LOW
    tokens = got.shape[2]
    rows = send.shape[1] // 2
    parts = hidden // width
    base = lax.axis_index("zl") * mine
    x_index = lax.axis_index("x")
    collect(got, 0, local, mixed)
    collect(got, 1, local, d_down)
    for b in range(mine):
        held = pl.ds(b * width, width)
        h = dot(w2[base + b], mixed[held, :], TN)
        squared = h * h
        half = 0.5 + 0.5 * jnp.tanh(h * (ROOT + (ROOT * CUBIC) * squared))
        act[b] = (h * half).astype(BF)
        gain = half + h * (half - half * half) * (2.0 * ROOT + (6.0 * ROOT * CUBIC) * squared)
        d_pre[b] = (dot(w3[base + b], d_down[held, :], NN) * gain).astype(BF)
    leaving = []
    for k, (w, value, dims) in enumerate(((w3, act, TN), (w2, d_pre, NN))):
        results = [dot(w[base + b], value[b], dims) for b in range(mine)]
        part = slice(k * rows, (k + 1) * rows)
        for zl in range(Z_LOW):
            cols = slice(zl * tokens, (zl + 1) * tokens)
            members = slice(zl * groups, (zl + 1) * groups)
            ready[members, part, :] = stack(*[z[:, cols] for z in results]).astype(BF)
        part = pl.ds(k * rows, rows)
        copy = pltpu.make_async_copy(ready.at[:, part, :], send.at[:, part, :], left.at[k])
        copy.start()
        leaving.append(copy)
    for b in range(mine):
        held = pl.ds(b * width, width)
        second = dot(mixed[held, :], d_pre[b], NT).astype(BF)
        for j in range(parts):
            part = slice(j * width, (j + 1) * width)
            grads[b, part, :] = second[:, part]
        grads[mine + b] = dot(act[b], d_down[held, :], NT).astype(BF)
    for k in range(X_SIZE):
        shares[k][...] = grads[(x_index + k) % X_SIZE]
    for copy in leaving:
        copy.wait()


def leave_kernel(got, x, dy, *rest):
    *shares, back, d_first, grads, wide_sum, ready, left = rest
    parts, width, _ = ready.shape
    local = parts // 2
    leaving = []

    def leave(k, value):
        ready[k] = value.astype(BF)
        copy = pltpu.make_async_copy(ready.at[k], grads.at[k], left.at[k])
        copy.start()
        leaving.append(copy)

    collect_back(got, 0, local, back)
    for b in range(local):
        rows = pl.ds(b * width, width)
        leave(local + b, dot(back[rows, :], dy[:, rows], NN))
    collect_back(got, 1, local, d_first)
    for b in range(local):
        rows = pl.ds(b * width, width)
        leave(b, dot(x[:, rows], d_first[rows, :], TT))
    acc = shares[0][...].astype(F32)
    for share in shares[1:]:
        acc = acc + share[...].astype(F32)
    wide_sum[...] = acc.astype(BF)
    for copy in leaving:
        copy.wait()


def outputs_kernel(back, d_first, w1, w4, output, grad_tokens):
    local, width, _ = w1.shape
    for b in range(local):
        cols = pl.ds(b * width, width)
        output[:, cols] = dot(back[cols, :], w4[b], TN).astype(BF)
        grad_tokens[:, cols] = dot(d_first[cols, :], w1[b], TT).astype(BF)


def add_kernel(got, wide_sum, total):
    high = wide_sum.shape[0]
    total[:high, :] = wide_sum[...]
    acc = got[0].astype(F32)
    for k in range(1, got.shape[0]):
        acc = acc + got[k].astype(F32)
    total[high:, :] = acc.astype(BF)


def add_copy_kernel(scale, got, copies):
    acc = got[0].astype(F32)
    for k in range(1, got.shape[0]):
        acc = acc + got[k].astype(F32)
    total = (acc * scale).astype(BF)
    for k in range(copies.shape[0]):
        copies[k] = total


def unpack_kernel(got, first, second, third, fourth):
    local, width, hidden = second.shape
    parts = hidden // width
    mine = local // Z_LOW
    for b in range(local):
        k = b // mine * X_SIZE + b % mine
        for j in range(parts):
            part = slice(j * width, (j + 1) * width)
            second[b, :, part] = got[k, part, :]
        third[b] = got[k + mine, :hidden, :]
        first[b] = got[b, hidden:, :]
        fourth[b] = got[local + b, hidden:, :]


def exchange(value, axes):
    return lax.all_to_all(value, axes, split_axis=0, concat_axis=0, tiled=True)


def body(all_tokens, tokens, w_first, w_second, w_third, w_fourth, upstream):
    count, wide = tokens.shape
    local, width, hidden = w_second.shape
    groups = lax.axis_size("hidden")
    near, middle = ("zl", "x"), ("zl", "hidden")
    parts = Z_LOW * X_SIZE
    mine = local // Z_LOW
    scale = float(all_tokens) ** -0.5
    rows = 2 * local * mine * PAIR
    entering = (tokens, w_first, upstream, w_fourth)
    (send,) = call(
        functools.partial(enter_kernel, groups),
        [shape(Z_LOW * groups, rows, count)],
        *entering,
        flops=4 * count * wide * width, vmem=60 << 20,
        in_specs=[pl.BlockSpec(memory_space=pltpu.HBM)] * 4,
        scratch_shapes=[pltpu.VMEM(a.shape, BF) for a in entering]
        + [pltpu.SemaphoreType.DMA((4,))],
    )
    got = exchange(send, middle)
    both = Z_LOW * count
    send, *shares = call(
        functools.partial(middle_kernel, groups),
        [shape(Z_LOW * groups, rows, count)] + [shape(hidden, width)] * X_SIZE,
        got, w_second, w_third,
        flops=12 * count * wide * hidden, transcendentals=count * local * hidden,
        scratch_shapes=[pltpu.VMEM((mine * width, both), BF)] * 2
        + [pltpu.VMEM((mine, hidden, both), BF)] * 2
        + [pltpu.VMEM((X_SIZE, hidden, width), BF), pltpu.VMEM(got.shape, BF)]
        + [pltpu.SemaphoreType.DMA((2,))],
        out_specs=[pl.BlockSpec(memory_space=pl.ANY)] + [pl.BlockSpec()] * X_SIZE,
    )
    got = exchange(send, middle)
    shares = [
        share if k == 0 else lax.ppermute(share, "x", [(i, (i + k) % X_SIZE) for i in range(X_SIZE)])
        for k, share in enumerate(shares)
    ]
    back, d_first, grads, wide_sum = call(
        leave_kernel,
        [
            shape(wide, count), shape(wide, count), shape(parts, width, width),
            shape(hidden, width),
        ],
        got, tokens, upstream, *shares,
        flops=8 * count * wide * width,
        out_specs=[
            pl.BlockSpec(), pl.BlockSpec(), pl.BlockSpec(memory_space=pl.ANY), pl.BlockSpec(),
        ],
        scratch_shapes=[
            pltpu.VMEM((parts, width, width), BF), pltpu.SemaphoreType.DMA((parts,)),
        ],
    )
    got = exchange(grads, near)
    output, grad_tokens = call(
        outputs_kernel, [shape(count, wide), shape(count, wide)],
        back, d_first, w_first, w_fourth,
        flops=4 * count * wide * width,
    )
    got, output, grad_tokens = lax.optimization_barrier((got, output, grad_tokens))
    (total,) = call(
        add_kernel, [shape(hidden + width, width)], got, wide_sum, flops=4 * hidden * width
    )
    got = lax.all_gather(total, "far", axis=0, tiled=False)
    (copies,) = call(
        functools.partial(add_copy_kernel, scale),
        [shape(parts, hidden + width, width)], got, flops=got.size,
    )
    got = exchange(copies, near)
    first, second, third, fourth = call(
        unpack_kernel,
        [shape(*w.shape) for w in (w_first, w_second, w_third, w_fourth)],
        got,
    )
    return output, grad_tokens, first, second, third, fourth


def solution(mesh):
    seq, groups = mesh.shape["seq"], mesh.shape["hidden"]
    fine = Mesh(
        mesh.devices.reshape(seq // (Z_LOW * X_SIZE), Z_LOW, X_SIZE, groups),
        ("far", "zl", "x", "hidden"),
    )
    rows = P(("far", "zl", "x"), "hidden")
    weight = P("hidden", None, None)

    def run(tokens, w_first, w_second, w_third, w_fourth, upstream):
        return jax.shard_map(
            functools.partial(body, tokens.shape[0]),
            mesh=fine,
            in_specs=(rows, weight, weight, weight, weight, rows),
            out_specs=(rows, rows, weight, weight, weight, weight),
            check_vma=False,
        )(tokens, w_first, w_second, w_third, w_fourth, upstream)

    return run
```

```python
import functools

import jax
import jax.numpy as jnp
from jax import lax
from jax.experimental import pallas as pl
from jax.experimental.pallas import tpu as pltpu
from jax.sharding import Mesh, PartitionSpec as P

ROOT = 0.7978845608
CUBIC = 0.044715
BF = jnp.bfloat16
F32 = jnp.float32
PAIR = 2
Z_LOW = 2
X_SIZE = 4
NN = (((1,), (0,)), ((), ()))
NT = (((1,), (1,)), ((), ()))
TN = (((0,), (0,)), ((), ()))
TT = (((0,), (1,)), ((), ()))


def dot(a, b, dims):
    return lax.dot_general(a, b, dims, preferred_element_type=F32)


def call(kernel, outs, *args, flops=0, transcendentals=0, vmem=24 << 20, **more):
    moved = sum(a.size * a.dtype.itemsize for a in (*args, *outs))
    return pl.pallas_call(
        kernel,
        out_shape=outs,
        compiler_params=pltpu.CompilerParams(vmem_limit_bytes=vmem),
        cost_estimate=pl.CostEstimate(
            flops=int(flops), bytes_accessed=int(moved), transcendentals=int(transcendentals)
        ),
        **more,
    )(*args)


def shape(*dims, dtype=BF):
    return jax.ShapeDtypeStruct(dims, dtype)


def stack(low, high):
    width, tokens = low.shape
    per = 2 * PAIR * Z_LOW
    split = (width // per, per, tokens)
    return jnp.concatenate([low.reshape(split), high.reshape(split)], axis=1)


def enter_kernel(groups, x_in, w1_in, dy_in, w4_in, out, x, w1, dy, w4, send, arrived, left):
    copies = [
        pltpu.make_async_copy(source, target, arrived.at[k])
        for k, (source, target) in enumerate(((x_in, x), (w1_in, w1), (dy_in, dy), (w4_in, w4)))
    ]
    for copy in copies:
        copy.start()
    local, width, _ = w1.shape
    tokens = x.shape[0]
    per = width // groups
    rows = local * per // Z_LOW
    leaving = []
    first_half = lax.broadcasted_iota(jnp.int32, (groups, per, tokens), 1) < per // 2
    for k in range(2):
        copies[2 * k].wait()
        copies[2 * k + 1].wait()
        to_zl = [[], []]
        for pair in range(local // 2):
            both = []
            for b in (2 * pair, 2 * pair + 1):
                cols = pl.ds(b * width, width)
                if k == 0:
                    z = dot(w1[b], x[:, cols], TT)
                else:
                    z = dot(w4[b], dy[:, cols], NT)
                both.append(z.reshape(groups, per, tokens))
            low, high = both
            to_zl[0].append(jnp.where(first_half, low, pltpu.roll(high, per // 2, 1)))
            to_zl[1].append(jnp.where(first_half, pltpu.roll(low, per // 2, 1), high))
        for zl in range(Z_LOW):
            filled = jnp.concatenate(to_zl[zl], axis=1).astype(BF)
            send[zl * groups : (zl + 1) * groups, k * rows : (k + 1) * rows, :] = filled
        part = pl.ds(k * rows, rows)
        copy = pltpu.make_async_copy(send.at[:, part, :], out.at[:, part, :], left.at[k])
        copy.start()
        leaving.append(copy)
    for copy in leaving:
        copy.wait()


def one_hot(source):
    n = source.shape[0]
    return (lax.broadcasted_iota(jnp.int32, (n, n), 1) == source).astype(F32).astype(BF)


def collect(got, k, theirs, out):
    count, rows, tokens = got.shape
    groups, held = count // Z_LOW, rows // 2
    mine = held // (theirs * PAIR)
    n = out.shape[0] // mine
    some = n // held
    per = theirs * PAIR
    r = lax.broadcasted_iota(jnp.int32, (n, 1), 0)
    own, group = r // (some * per), (r // per) % some
    their, one = (r // PAIR) % theirs, r % PAIR
    order = one_hot(group * held + their * (mine * PAIR) + own * PAIR + one)
    for zl in range(Z_LOW):
        for g in range(groups // some):
            at = zl * groups + g * some
            taken = got[at : at + some, k * held : (k + 1) * held, :].reshape(n, tokens)
            moved = dot(order, taken, NN).astype(BF)
            for b in range(mine):
                to = b * n + g * some * per
                out[to : to + some * per, zl * tokens : (zl + 1) * tokens] = moved[
                    b * some * per : (b + 1) * some * per, :
                ]


def collect_back(got, k, local, out):
    count, rows, tokens = got.shape
    groups, held = count // Z_LOW, rows // 2
    theirs = held // (local * PAIR)
    n = out.shape[0] // local
    some = n // (Z_LOW * held)
    per = Z_LOW * theirs * PAIR
    r = lax.broadcasted_iota(jnp.int32, (n, 1), 0)
    own, group = r // (some * per), (r // per) % some
    zl, their, one = (r // (theirs * PAIR)) % Z_LOW, (r // PAIR) % theirs, r % PAIR
    order = one_hot((zl * some + group) * held + their * (local * PAIR) + own * PAIR + one)
    for g in range(groups // some):
        taken = jnp.concatenate(
            [
                got[z * groups + g * some : z * groups + (g + 1) * some, k * held : (k + 1) * held, :]
                .reshape(some * held, tokens)
                for z in range(Z_LOW)
            ],
            axis=0,
        )
        moved = dot(order, taken, NN).astype(BF)
        for b in range(local):
            to = b * n + g * some * per
            out[to : to + some * per, :] = moved[b * some * per : (b + 1) * some * per, :]


def middle_kernel(groups, got, w2, w3, send, *rest):
    shares, (mixed, d_down, act, d_pre, grads, ready, left) = rest[:X_SIZE], rest[X_SIZE:]
    local, width, hidden = w2.shape
    mine = local // Z_LOW
    tokens = got.shape[2]
    rows = send.shape[1] // 2
    parts = hidden // width
    base = lax.axis_index("zl") * mine
    x_index = lax.axis_index("x")
    collect(got, 0, local, mixed)
    collect(got, 1, local, d_down)
    for b in range(mine):
        held = pl.ds(b * width, width)
        h = dot(w2[base + b], mixed[held, :], TN)
        squared = h * h
        half = 0.5 + 0.5 * jnp.tanh(h * (ROOT + (ROOT * CUBIC) * squared))
        act[b] = (h * half).astype(BF)
        gain = half + h * (half - half * half) * (2.0 * ROOT + (6.0 * ROOT * CUBIC) * squared)
        d_pre[b] = (dot(w3[base + b], d_down[held, :], NN) * gain).astype(BF)
    leaving = []
    for k, (w, value, dims) in enumerate(((w3, act, TN), (w2, d_pre, NN))):
        results = [dot(w[base + b], value[b], dims) for b in range(mine)]
        part = slice(k * rows, (k + 1) * rows)
        for zl in range(Z_LOW):
            cols = slice(zl * tokens, (zl + 1) * tokens)
            members = slice(zl * groups, (zl + 1) * groups)
            ready[members, part, :] = stack(*[z[:, cols] for z in results]).astype(BF)
        part = pl.ds(k * rows, rows)
        copy = pltpu.make_async_copy(ready.at[:, part, :], send.at[:, part, :], left.at[k])
        copy.start()
        leaving.append(copy)
    for b in range(mine):
        held = pl.ds(b * width, width)
        second = dot(mixed[held, :], d_pre[b], NT).astype(BF)
        for j in range(parts):
            part = slice(j * width, (j + 1) * width)
            grads[b, part, :] = second[:, part]
        grads[mine + b] = dot(act[b], d_down[held, :], NT).astype(BF)
    for k in range(X_SIZE):
        shares[k][...] = grads[(x_index + k) % X_SIZE]
    for copy in leaving:
        copy.wait()


def leave_kernel(got, x, dy, *rest):
    *shares, back, d_first, grads, wide_sum, ready, left = rest
    parts, width, _ = ready.shape
    local = parts // 2
    leaving = []

    def leave(k, value):
        ready[k] = value.astype(BF)
        copy = pltpu.make_async_copy(ready.at[k], grads.at[k], left.at[k])
        copy.start()
        leaving.append(copy)

    collect_back(got, 0, local, back)
    for b in range(local):
        rows = pl.ds(b * width, width)
        leave(local + b, dot(back[rows, :], dy[:, rows], NN))
    collect_back(got, 1, local, d_first)
    for b in range(local):
        rows = pl.ds(b * width, width)
        leave(b, dot(x[:, rows], d_first[rows, :], TT))
    acc = shares[0][...].astype(F32)
    for share in shares[1:]:
        acc = acc + share[...].astype(F32)
    wide_sum[...] = acc.astype(BF)
    for copy in leaving:
        copy.wait()


def outputs_kernel(back, d_first, w1, w4, output, grad_tokens):
    local, width, _ = w1.shape
    for b in range(local):
        cols = pl.ds(b * width, width)
        output[:, cols] = dot(back[cols, :], w4[b], TN).astype(BF)
        grad_tokens[:, cols] = dot(d_first[cols, :], w1[b], TT).astype(BF)


def add_kernel(got, wide_sum, total):
    high = wide_sum.shape[0]
    total[:high, :] = wide_sum[...]
    acc = got[0].astype(F32)
    for k in range(1, got.shape[0]):
        acc = acc + got[k].astype(F32)
    total[high:, :] = acc.astype(BF)


def add_copy_kernel(scale, got, copies):
    acc = got[0].astype(F32)
    for k in range(1, got.shape[0]):
        acc = acc + got[k].astype(F32)
    total = (acc * scale).astype(BF)
    for k in range(copies.shape[0]):
        copies[k] = total


def unpack_kernel(got, first, second, third, fourth):
    local, width, hidden = second.shape
    parts = hidden // width
    mine = local // Z_LOW
    for b in range(local):
        k = b // mine * X_SIZE + b % mine
        for j in range(parts):
            part = slice(j * width, (j + 1) * width)
            second[b, :, part] = got[k, part, :]
        third[b] = got[k + mine, :hidden, :]
        first[b] = got[b, hidden:, :]
        fourth[b] = got[local + b, hidden:, :]


def exchange(value, axes):
    return lax.all_to_all(value, axes, split_axis=0, concat_axis=0, tiled=True)


def body(all_tokens, tokens, w_first, w_second, w_third, w_fourth, upstream):
    count, wide = tokens.shape
    local, width, hidden = w_second.shape
    groups = lax.axis_size("hidden")
    near, middle = ("zl", "x"), ("zl", "hidden")
    parts = Z_LOW * X_SIZE
    mine = local // Z_LOW
    scale = float(all_tokens) ** -0.5
    rows = 2 * local * mine * PAIR
    entering = (tokens, w_first, upstream, w_fourth)
    (send,) = call(
        functools.partial(enter_kernel, groups),
        [shape(Z_LOW * groups, rows, count)],
        *entering,
        flops=4 * count * wide * width, vmem=60 << 20,
        in_specs=[pl.BlockSpec(memory_space=pltpu.HBM)] * 4,
        out_specs=[pl.BlockSpec(memory_space=pl.ANY)],
        scratch_shapes=[pltpu.VMEM(a.shape, BF) for a in entering]
        + [pltpu.VMEM((Z_LOW * groups, rows, count), BF)]
        + [pltpu.SemaphoreType.DMA((4,)), pltpu.SemaphoreType.DMA((2,))],
    )
    got = exchange(send, middle)
    both = Z_LOW * count
    send, *shares = call(
        functools.partial(middle_kernel, groups),
        [shape(Z_LOW * groups, rows, count)] + [shape(hidden, width)] * X_SIZE,
        got, w_second, w_third,
        flops=12 * count * wide * hidden, transcendentals=count * local * hidden,
        scratch_shapes=[pltpu.VMEM((mine * width, both), BF)] * 2
        + [pltpu.VMEM((mine, hidden, both), BF)] * 2
        + [pltpu.VMEM((X_SIZE, hidden, width), BF), pltpu.VMEM(got.shape, BF)]
        + [pltpu.SemaphoreType.DMA((2,))],
        out_specs=[pl.BlockSpec(memory_space=pl.ANY)] + [pl.BlockSpec()] * X_SIZE,
    )
    got = exchange(send, middle)
    shares = [
        share if k == 0 else lax.ppermute(share, "x", [(i, (i + k) % X_SIZE) for i in range(X_SIZE)])
        for k, share in enumerate(shares)
    ]
    back, d_first, grads, wide_sum = call(
        leave_kernel,
        [
            shape(wide, count), shape(wide, count), shape(parts, width, width),
            shape(hidden, width),
        ],
        got, tokens, upstream, *shares,
        flops=8 * count * wide * width,
        out_specs=[
            pl.BlockSpec(), pl.BlockSpec(), pl.BlockSpec(memory_space=pl.ANY), pl.BlockSpec(),
        ],
        scratch_shapes=[
            pltpu.VMEM((parts, width, width), BF), pltpu.SemaphoreType.DMA((parts,)),
        ],
    )
    got = exchange(grads, near)
    output, grad_tokens = call(
        outputs_kernel, [shape(count, wide), shape(count, wide)],
        back, d_first, w_first, w_fourth,
        flops=4 * count * wide * width,
    )
    got, output, grad_tokens = lax.optimization_barrier((got, output, grad_tokens))
    (total,) = call(
        add_kernel, [shape(hidden + width, width)], got, wide_sum, flops=4 * hidden * width
    )
    got = lax.all_gather(total, "far", axis=0, tiled=False)
    (copies,) = call(
        functools.partial(add_copy_kernel, scale),
        [shape(parts, hidden + width, width)], got, flops=got.size,
    )
    got = exchange(copies, near)
    first, second, third, fourth = call(
        unpack_kernel,
        [shape(*w.shape) for w in (w_first, w_second, w_third, w_fourth)],
        got,
    )
    return output, grad_tokens, first, second, third, fourth


def solution(mesh):
    seq, groups = mesh.shape["seq"], mesh.shape["hidden"]
    fine = Mesh(
        mesh.devices.reshape(seq // (Z_LOW * X_SIZE), Z_LOW, X_SIZE, groups),
        ("far", "zl", "x", "hidden"),
    )
    rows = P(("far", "zl", "x"), "hidden")
    weight = P("hidden", None, None)

    def run(tokens, w_first, w_second, w_third, w_fourth, upstream):
        return jax.shard_map(
            functools.partial(body, tokens.shape[0]),
            mesh=fine,
            in_specs=(rows, weight, weight, weight, weight, rows),
            out_specs=(rows, rows, weight, weight, weight, weight),
            check_vma=False,
        )(tokens, w_first, w_second, w_third, w_fourth, upstream)

    return run
```

```python
import functools

import jax
import jax.numpy as jnp
from jax import lax
from jax.experimental import pallas as pl
from jax.experimental.pallas import tpu as pltpu
from jax.sharding import Mesh, PartitionSpec as P

ROOT = 0.7978845608
CUBIC = 0.044715
BF = jnp.bfloat16
F32 = jnp.float32
PAIR = 2
Z_LOW = 2
X_SIZE = 4
NN = (((1,), (0,)), ((), ()))
NT = (((1,), (1,)), ((), ()))
TN = (((0,), (0,)), ((), ()))
TT = (((0,), (1,)), ((), ()))


def dot(a, b, dims):
    return lax.dot_general(a, b, dims, preferred_element_type=F32)


def call(kernel, outs, *args, flops=0, transcendentals=0, vmem=24 << 20, **more):
    moved = sum(a.size * a.dtype.itemsize for a in (*args, *outs))
    return pl.pallas_call(
        kernel,
        out_shape=outs,
        compiler_params=pltpu.CompilerParams(vmem_limit_bytes=vmem),
        cost_estimate=pl.CostEstimate(
            flops=int(flops), bytes_accessed=int(moved), transcendentals=int(transcendentals)
        ),
        **more,
    )(*args)


def shape(*dims, dtype=BF):
    return jax.ShapeDtypeStruct(dims, dtype)


def stack(low, high):
    width, tokens = low.shape
    per = 2 * PAIR * Z_LOW
    split = (width // per, per, tokens)
    return jnp.concatenate([low.reshape(split), high.reshape(split)], axis=1)


def enter_kernel(groups, x_in, w1_in, dy_in, w4_in, out, x, w1, dy, w4, send, arrived, left):
    copies = [
        pltpu.make_async_copy(source, target, arrived.at[k])
        for k, (source, target) in enumerate(((x_in, x), (w1_in, w1), (dy_in, dy), (w4_in, w4)))
    ]
    for copy in copies:
        copy.start()
    local, width, _ = w1.shape
    tokens = x.shape[0]
    per = width // groups
    rows = local * per // Z_LOW
    leaving = []
    first_half = lax.broadcasted_iota(jnp.int32, (groups, per, tokens), 1) < per // 2
    for k in range(2):
        copies[2 * k].wait()
        copies[2 * k + 1].wait()
        to_zl = [[], []]
        for pair in range(local // 2):
            both = []
            for b in (2 * pair, 2 * pair + 1):
                cols = pl.ds(b * width, width)
                if k == 0:
                    z = dot(w1[b], x[:, cols], TT)
                else:
                    z = dot(w4[b], dy[:, cols], NT)
                both.append(z.reshape(groups, per, tokens))
            low, high = both
            to_zl[0].append(jnp.where(first_half, low, pltpu.roll(high, per // 2, 1)))
            to_zl[1].append(jnp.where(first_half, pltpu.roll(low, per // 2, 1), high))
        for zl in range(Z_LOW):
            filled = jnp.concatenate(to_zl[zl], axis=1).astype(BF)
            send[zl * groups : (zl + 1) * groups, k * rows : (k + 1) * rows, :] = filled
        part = pl.ds(k * rows, rows)
        copy = pltpu.make_async_copy(send.at[:, part, :], out.at[:, part, :], left.at[k])
        copy.start()
        leaving.append(copy)
    for copy in leaving:
        copy.wait()


def one_hot(source):
    n = source.shape[0]
    return (lax.broadcasted_iota(jnp.int32, (n, n), 1) == source).astype(F32).astype(BF)


def collect(got, k, theirs, out):
    count, rows, tokens = got.shape
    groups, held = count // Z_LOW, rows // 2
    mine = held // (theirs * PAIR)
    n = out.shape[0] // mine
    some = n // held
    per = theirs * PAIR
    r = lax.broadcasted_iota(jnp.int32, (n, 1), 0)
    own, group = r // (some * per), (r // per) % some
    their, one = (r // PAIR) % theirs, r % PAIR
    order = one_hot(group * held + their * (mine * PAIR) + own * PAIR + one)
    for zl in range(Z_LOW):
        for g in range(groups // some):
            at = zl * groups + g * some
            taken = got[at : at + some, k * held : (k + 1) * held, :].reshape(n, tokens)
            moved = dot(order, taken, NN).astype(BF)
            for b in range(mine):
                to = b * n + g * some * per
                out[to : to + some * per, zl * tokens : (zl + 1) * tokens] = moved[
                    b * some * per : (b + 1) * some * per, :
                ]


def collect_back(got, k, local, out):
    count, rows, tokens = got.shape
    groups, held = count // Z_LOW, rows // 2
    theirs = held // (local * PAIR)
    n = out.shape[0] // local
    some = n // (Z_LOW * held)
    per = Z_LOW * theirs * PAIR
    r = lax.broadcasted_iota(jnp.int32, (n, 1), 0)
    own, group = r // (some * per), (r // per) % some
    zl, their, one = (r // (theirs * PAIR)) % Z_LOW, (r // PAIR) % theirs, r % PAIR
    order = one_hot((zl * some + group) * held + their * (local * PAIR) + own * PAIR + one)
    for g in range(groups // some):
        taken = jnp.concatenate(
            [
                got[z * groups + g * some : z * groups + (g + 1) * some, k * held : (k + 1) * held, :]
                .reshape(some * held, tokens)
                for z in range(Z_LOW)
            ],
            axis=0,
        )
        moved = dot(order, taken, NN).astype(BF)
        for b in range(local):
            to = b * n + g * some * per
            out[to : to + some * per, :] = moved[b * some * per : (b + 1) * some * per, :]


def middle_kernel(groups, got, w2, w3, send, *rest):
    shares, (mixed, d_down, act, d_pre, grads, ready, left) = rest[:X_SIZE], rest[X_SIZE:]
    local, width, hidden = w2.shape
    mine = local // Z_LOW
    tokens = got.shape[2]
    rows = send.shape[1] // 2
    parts = hidden // width
    base = lax.axis_index("zl") * mine
    x_index = lax.axis_index("x")
    collect(got, 0, local, mixed)
    collect(got, 1, local, d_down)
    for b in range(mine):
        held = pl.ds(b * width, width)
        h = dot(w2[base + b], mixed[held, :], TN)
        squared = h * h
        half = 0.5 + 0.5 * jnp.tanh(h * (ROOT + (ROOT * CUBIC) * squared))
        act[b] = (h * half).astype(BF)
        gain = half + h * (half - half * half) * (2.0 * ROOT + (6.0 * ROOT * CUBIC) * squared)
        d_pre[b] = (dot(w3[base + b], d_down[held, :], NN) * gain).astype(BF)
    leaving = []
    for k, (w, value, dims) in enumerate(((w3, act, TN), (w2, d_pre, NN))):
        results = [dot(w[base + b], value[b], dims) for b in range(mine)]
        part = slice(k * rows, (k + 1) * rows)
        for zl in range(Z_LOW):
            cols = slice(zl * tokens, (zl + 1) * tokens)
            members = slice(zl * groups, (zl + 1) * groups)
            ready[members, part, :] = stack(*[z[:, cols] for z in results]).astype(BF)
        part = pl.ds(k * rows, rows)
        copy = pltpu.make_async_copy(ready.at[:, part, :], send.at[:, part, :], left.at[k])
        copy.start()
        leaving.append(copy)
    for b in range(mine):
        held = pl.ds(b * width, width)
        second = dot(mixed[held, :], d_pre[b], NT).astype(BF)
        for j in range(parts):
            part = slice(j * width, (j + 1) * width)
            grads[b, part, :] = second[:, part]
        grads[mine + b] = dot(act[b], d_down[held, :], NT).astype(BF)
    for k in range(X_SIZE):
        shares[k][...] = grads[(x_index + k) % X_SIZE]
    for copy in leaving:
        copy.wait()


def leave_kernel(got, x, dy, *rest):
    *shares, back, d_first, grads, wide_sum, ready, left = rest
    parts, width, _ = ready.shape
    local = parts // 2
    leaving = []

    def leave(k, value):
        ready[k] = value.astype(BF)
        copy = pltpu.make_async_copy(ready.at[k], grads.at[k], left.at[k])
        copy.start()
        leaving.append(copy)

    collect_back(got, 0, local, back)
    for b in range(local):
        rows = pl.ds(b * width, width)
        leave(local + b, dot(back[rows, :], dy[:, rows], NN))
    collect_back(got, 1, local, d_first)
    for b in range(local):
        rows = pl.ds(b * width, width)
        leave(b, dot(x[:, rows], d_first[rows, :], TT))
    acc = shares[0][...].astype(F32)
    for share in shares[1:]:
        acc = acc + share[...].astype(F32)
    wide_sum[...] = acc.astype(BF)
    for copy in leaving:
        copy.wait()


def outputs_kernel(back, d_first, w1, w4, output, grad_tokens):
    local, width, _ = w1.shape
    for b in range(local):
        cols = pl.ds(b * width, width)
        output[:, cols] = dot(back[cols, :], w4[b], TN).astype(BF)
        grad_tokens[:, cols] = dot(d_first[cols, :], w1[b], TT).astype(BF)


def add_kernel(got, wide_sum, total):
    high = wide_sum.shape[0]
    total[:high, :] = wide_sum[...]
    acc = got[0].astype(F32)
    for k in range(1, got.shape[0]):
        acc = acc + got[k].astype(F32)
    total[high:, :] = acc.astype(BF)


def add_copy_kernel(scale, got, copies):
    acc = got[0].astype(F32)
    for k in range(1, got.shape[0]):
        acc = acc + got[k].astype(F32)
    total = (acc * scale).astype(BF)
    for k in range(copies.shape[0]):
        copies[k] = total


def unpack_kernel(got, first, second, third, fourth):
    local, width, hidden = second.shape
    parts = hidden // width
    mine = local // Z_LOW
    for b in range(local):
        k = b // mine * X_SIZE + b % mine
        for j in range(parts):
            part = slice(j * width, (j + 1) * width)
            second[b, :, part] = got[k, part, :]
        third[b] = got[k + mine, :hidden, :]
        first[b] = got[b, hidden:, :]
        fourth[b] = got[local + b, hidden:, :]


def exchange(value, axes):
    return lax.all_to_all(value, axes, split_axis=0, concat_axis=0, tiled=True)


def body(all_tokens, tokens, w_first, w_second, w_third, w_fourth, upstream):
    count, wide = tokens.shape
    local, width, hidden = w_second.shape
    groups = lax.axis_size("hidden")
    near, middle = ("zl", "x"), ("zl", "hidden")
    parts = Z_LOW * X_SIZE
    mine = local // Z_LOW
    scale = float(all_tokens) ** -0.5
    rows = 2 * local * mine * PAIR
    entering = (tokens, w_first, upstream, w_fourth)
    (send,) = call(
        functools.partial(enter_kernel, groups),
        [shape(Z_LOW * groups, rows, count)],
        *entering,
        flops=4 * count * wide * width, vmem=60 << 20,
        in_specs=[pl.BlockSpec(memory_space=pltpu.HBM)] * 4,
        out_specs=[pl.BlockSpec(memory_space=pl.ANY)],
        scratch_shapes=[pltpu.VMEM(a.shape, BF) for a in entering]
        + [pltpu.VMEM((Z_LOW * groups, rows, count), BF)]
        + [pltpu.SemaphoreType.DMA((4,)), pltpu.SemaphoreType.DMA((2,))],
    )
    got = exchange(send, middle)
    both = Z_LOW * count
    send, *shares = call(
        functools.partial(middle_kernel, groups),
        [shape(Z_LOW * groups, rows, count)] + [shape(hidden, width)] * X_SIZE,
        got, w_second, w_third,
        flops=12 * count * wide * hidden, transcendentals=count * local * hidden,
        scratch_shapes=[pltpu.VMEM((mine * width, both), BF)] * 2
        + [pltpu.VMEM((mine, hidden, both), BF)] * 2
        + [pltpu.VMEM((X_SIZE, hidden, width), BF), pltpu.VMEM(got.shape, BF)]
        + [pltpu.SemaphoreType.DMA((2,))],
        out_specs=[pl.BlockSpec(memory_space=pl.ANY)] + [pl.BlockSpec()] * X_SIZE,
    )
    got = exchange(send, middle)
    shares = shares[:1] + [
        lax.ppermute(shares[k], "x", [(i, (i + k) % X_SIZE) for i in range(X_SIZE)])
        for k in (2, 1, 3)
    ]
    back, d_first, grads, wide_sum = call(
        leave_kernel,
        [
            shape(wide, count), shape(wide, count), shape(parts, width, width),
            shape(hidden, width),
        ],
        got, tokens, upstream, *shares,
        flops=8 * count * wide * width,
        out_specs=[
            pl.BlockSpec(), pl.BlockSpec(), pl.BlockSpec(memory_space=pl.ANY), pl.BlockSpec(),
        ],
        scratch_shapes=[
            pltpu.VMEM((parts, width, width), BF), pltpu.SemaphoreType.DMA((parts,)),
        ],
    )
    got = exchange(grads, near)
    output, grad_tokens = call(
        outputs_kernel, [shape(count, wide), shape(count, wide)],
        back, d_first, w_first, w_fourth,
        flops=4 * count * wide * width,
    )
    got, output, grad_tokens = lax.optimization_barrier((got, output, grad_tokens))
    (total,) = call(
        add_kernel, [shape(hidden + width, width)], got, wide_sum, flops=4 * hidden * width
    )
    got = lax.all_gather(total, "far", axis=0, tiled=False)
    (copies,) = call(
        functools.partial(add_copy_kernel, scale),
        [shape(parts, hidden + width, width)], got, flops=got.size,
    )
    got = exchange(copies, near)
    first, second, third, fourth = call(
        unpack_kernel,
        [shape(*w.shape) for w in (w_first, w_second, w_third, w_fourth)],
        got,
    )
    return output, grad_tokens, first, second, third, fourth


def solution(mesh):
    seq, groups = mesh.shape["seq"], mesh.shape["hidden"]
    fine = Mesh(
        mesh.devices.reshape(seq // (Z_LOW * X_SIZE), Z_LOW, X_SIZE, groups),
        ("far", "zl", "x", "hidden"),
    )
    rows = P(("far", "zl", "x"), "hidden")
    weight = P("hidden", None, None)

    def run(tokens, w_first, w_second, w_third, w_fourth, upstream):
        return jax.shard_map(
            functools.partial(body, tokens.shape[0]),
            mesh=fine,
            in_specs=(rows, weight, weight, weight, weight, rows),
            out_specs=(rows, rows, weight, weight, weight, weight),
            check_vma=False,
        )(tokens, w_first, w_second, w_third, w_fourth, upstream)

    return run
```
